32 devices in a mesh: group: 2 (over x), ctx: 16 (over z, y, core).
Axes of the slice: x: 2, y: 2, z: 4, core: 2. Of those that a mesh axis runs over, the one named last changes fastest.
Arguments:
- signal: bfloat16 [32768, 256], P(('group', 'ctx')), parts along dimension 0, may hold values from -6 to 6
- gate_one: bfloat16 [32768, 256], P(('group', 'ctx')), parts along dimension 0, may hold values from -6 to 6
- mix_two: bfloat16 [32768, 256], P(('group', 'ctx')), parts along dimension 0, may hold values from -6 to 6
- gate_two: bfloat16 [32768, 256], P(('group', 'ctx')), parts along dimension 0, may hold values from -6 to 6
- skip_one: float32 [256], replicated, may hold values from 0.5 to 1.5
- skip_two: float32 [256], replicated, may hold values from 0.5 to 1.5
- spectrum_one: bfloat16 [2, 32, 1024, 256], P(None, 'ctx'), may hold values from -6 to 6, as said below
- spectrum_two: bfloat16 [2, 32, 1024, 256], P(None, 'ctx'), may hold values from -6 to 6, as said below
Outputs:
- response: bfloat16 [32768, 256], P(('group', 'ctx')), parts along dimension 0
The draws below stay inside these ranges and needn't reach their ends.
There are 2 independent parts, one for each index of `group`. The reference program is written for one: setup_inputs(seed, part) draws one part's arguments, and reference() takes and returns one part's arrays. A program takes and returns all parts, laid end to end along the dimension named above; an argument that names none is the same for every part. Nothing has to cross between parts.
Inputs may be any that keep to these rules, and one draw needn't show every extreme that they name: `spectrum_one`: the spectrum is Hermitian, as that of a real filter: H[32768 - k] is the complex conjugate of H[k]; H[0] and H[16384] are real. `spectrum_two`: the spectrum is Hermitian, as that of a real filter: H[32768 - k] is the complex conjugate of H[k]; H[0] and H[16384] are real.
All inputs are finite; a program needn't handle non-finite values.
Results may differ from the reference program's by a relative error of at most 0.0049.
Values may be sent and summed in bfloat16 or wider, within the bound.
No kernel may reach another device: no remote copies, remote signals or barrier semaphores. Data moves between devices by JAX's collectives and lax.ppermute only.
A program may use at most 128 MiB of HBM per device.

```python
import jax
import jax.numpy as jnp
from jax import lax

CH = 256
TOK_DEV = 1024
SEQ = 16384
N_CTX = 16


def hermitian_layout(raw):
    mirror = jnp.roll(jnp.flip(raw, 1), 1, 1)
    real_part = (raw[0] + mirror[0]) * 0.5
    imag_part = (raw[1] - mirror[1]) * 0.5
    stacked = jnp.stack([real_part, imag_part]).reshape(2, TOK_DEV, 2 * N_CTX, CH)
    return jnp.transpose(stacked, (0, 2, 1, 3)).astype(jnp.bfloat16)


def draw_spectrum_one(key, part):
    key = jax.random.fold_in(key, 11)
    shape_full = (2, 2 * TOK_DEV * N_CTX, CH)
    raw = jnp.clip(jax.random.normal(key, shape_full, jnp.float32), -6.0, 6.0)
    return hermitian_layout(raw)


def draw_spectrum_two(key, part):
    key = jax.random.fold_in(key, 23)
    shape_full = (2, 2 * TOK_DEV * N_CTX, CH)
    raw = jnp.clip(jax.random.normal(key, shape_full, jnp.float32), -6.0, 6.0)
    return hermitian_layout(raw)


def levels(rng, dims, pieces, smallest, top_value):
    gain, own = 1.0, jax.random.fold_in(rng, 6)
    for position, parts in pieces:
        steps = jnp.exp(jax.random.uniform(jax.random.fold_in(own, position), (parts,), jnp.float32, smallest / len(pieces), top_value / len(pieces)))
        gain = gain * jnp.repeat(steps, dims[position] // parts).reshape([-1 if axis == position else 1 for axis in range(len(dims))])
    return gain


def gaussian(rng, extent, spread, most, split=(), kind=jnp.bfloat16):
    array = jax.random.normal(rng, extent, jnp.float32) * spread
    if len(split) > 0:
        array = levels(rng, extent, split, -0.22, 0.18) * array
    return jnp.clip(array, min=-most, max=most).astype(kind)


def setup_inputs(seed: int = 0, part: int = 0) -> dict:
    seeds = jax.random.split(jax.random.key(seed), 9)
    part_keys = jax.random.split(jax.random.fold_in(seeds[8], part), 9)
    return {
        "signal": gaussian(part_keys[0], (SEQ, CH), 1.0, 6.0, ((0, 16),)),
        "gate_one": gaussian(part_keys[1], (SEQ, CH), 1.0, 6.0, ((0, 16),)),
        "mix_two": gaussian(part_keys[2], (SEQ, CH), 1.0, 6.0, ((0, 16),)),
        "gate_two": gaussian(part_keys[3], (SEQ, CH), 1.0, 6.0, ((0, 16),)),
        "skip_one": jnp.clip(jax.random.uniform(seeds[4], (CH,), jnp.float32, 0.5, 1.5), 0.5, 1.5),
        "skip_two": jnp.clip(jax.random.uniform(seeds[5], (CH,), jnp.float32, 0.5, 1.5), 0.5, 1.5),
        "spectrum_one": draw_spectrum_one(jax.random.fold_in(seeds[8], 71), part),
        "spectrum_two": draw_spectrum_two(jax.random.fold_in(seeds[8], 71), part),
    }


def convolve(field, spectrum):
    seq_len = field.shape[0]
    channels = field.shape[1]
    padded = jnp.concatenate([field, jnp.zeros_like(field)], axis=0)
    freq_all = jnp.fft.fft(padded, axis=0)
    spec_full = spectrum.astype(jnp.float32)
    natural = jnp.transpose(spec_full, (0, 2, 1, 3)).reshape(2, 2 * seq_len, channels)
    product = freq_all * lax.complex(natural[0], natural[1])
    return jnp.real(jnp.fft.ifft(product, axis=0))[:seq_len]


def reference(signal, gate_one, mix_two, gate_two, skip_one, skip_two, spectrum_one, spectrum_two):
    source = signal.astype(jnp.float32)
    first = convolve(source, spectrum_one)
    middle = (gate_one.astype(jnp.float32) * (first + skip_one * source) * mix_two.astype(jnp.float32)).astype(jnp.bfloat16)
    middle_f = middle.astype(jnp.float32)
    second = convolve(middle_f, spectrum_two)
    return (gate_two.astype(jnp.float32) * (second + skip_two * middle_f)).astype(jnp.bfloat16)
```

```python
import functools

import jax
import jax.numpy as jnp
import numpy as np
from jax import lax
from jax.experimental import pallas as pl
from jax.experimental.pallas import tpu as pltpu
from jax.sharding import PartitionSpec as P

F32 = jnp.float32
BF16 = jnp.bfloat16
LANES = 128
GROUP = 4
PARAMS = pltpu.CompilerParams(vmem_limit_bytes=48 * 1024 * 1024)


def split_table(table):
    high = table.astype(jnp.bfloat16)
    low = (table - high.astype(np.float64)).astype(jnp.bfloat16)
    return high, low


def make_tables(n, step):
    rows = n * step
    first_len = 2 * rows
    total = first_len * LANES
    turn = 2.0 * np.pi
    n1 = np.arange(rows)
    n2 = np.arange(LANES)
    forward_one, inverse_one, cosines, sines = [], [], [], []
    for half in range(2):
        k1 = np.array(
            [
                2 * (half * (n // 2) + source) + a + 2 * n * low
                for source in range(n // 2)
                for a in range(2)
                for low in range(step)
            ]
        )
        k1[:step] = [2 * n * j for j in range(step // 2)] + [n + 2 * n * j for j in range(step // 2)]
        angle = turn * ((k1[:, None] * n1[None, :]) % first_len) / first_len
        real_rows, imag_rows = np.cos(angle), -np.sin(angle)
        imag_rows[0] = np.cos(np.pi * n1)
        table = np.concatenate([real_rows, imag_rows], axis=0)
        forward_one.append(table)
        weight = np.full((2 * rows, 1), 2.0 / total)
        weight[0] = weight[rows] = 1.0 / total
        inverse_one.append((table * weight).T)
        angle = turn * ((k1[:, None] * n2[None, :]) % total) / total
        angle[0] = 0.0
        cosines.append(np.cos(angle))
        sines.append(-np.sin(angle))
    angle = turn * ((n2[:, None] * n2[None, :]) % LANES) / LANES
    cosine, sine = np.cos(angle), np.sin(angle)
    forward_two = np.block([[cosine, -sine], [sine, cosine]])
    inverse_two = np.block([[cosine, sine], [-sine, cosine]])
    half_lanes = LANES // 2
    even = turn * ((n2[:, None] * np.arange(half_lanes)[None, :]) % LANES) / LANES
    odd = turn * ((n2[:, None] * (1 + 2 * np.arange(half_lanes))[None, :]) % (2 * LANES)) / (2 * LANES)
    zero = np.zeros((LANES, half_lanes))
    even_imag = -np.sin(even)
    even_imag[:, 0] = np.cos(np.pi * n2)
    forward_row = np.block(
        [[np.cos(even), zero, even_imag, zero], [zero, np.cos(odd), zero, -np.sin(odd)]]
    )
    weight = np.full((2 * LANES, 1), 2.0)
    weight[0] = weight[LANES] = 1.0
    inverse_row = (forward_row * weight[:, 0][None, :]).T

    def along_rows(table):
        high, low = split_table(table)
        return np.concatenate([high, low, high], axis=0)

    def along_columns(table):
        high, low = split_table(table)
        return np.concatenate([high, low, high], axis=1)

    def two_columns(table):
        return np.concatenate(split_table(table), axis=1)

    return {
        "forward_one": np.stack([two_columns(t) for t in forward_one]),
        "inverse_one": np.stack([along_columns(t) for t in inverse_one]),
        "cosine": np.stack(cosines).astype(np.float32),
        "sine": np.stack(sines).astype(np.float32),
        "forward_two": along_rows(forward_two),
        "inverse_two": along_rows(inverse_two),
        "forward_row": along_rows(forward_row),
        "inverse_row": along_rows(inverse_row),
    }


def prep_kernel(scalars, signal, gate, mix, spec_one, spec_two, data, special, turned, strided):
    step = signal.shape[0] // LANES
    channels = signal.shape[1]
    devices = data.shape[0]
    rows = data.shape[1] // 2
    for part in range(2):
        for t in range(step):
            piece = pl.ds(t * LANES, LANES)
            if part == 0:
                value = signal[piece, :].astype(F32)
            else:
                value = gate[piece, :].astype(F32) * mix[piece, :].astype(F32)
            turned[pl.ds(t, channels, stride=step), :] = value.T
        data[:, part * rows : (part + 1) * rows, :] = (
            turned[...].reshape(devices, rows, LANES).astype(BF16)
        )
    is_first = scalars[3] == 1
    for index, spec in enumerate((spec_one, spec_two)):
        for ri in range(2):
            strided[ri] = spec[ri, 0].astype(F32)
        for j in range(step // 2):
            real_part, imag_part = (
                strided[ri, pl.ds(j, LANES, stride=step), :] for ri in range(2)
            )
            if j == 0:
                packed = pack_row(strided, real_part, imag_part, step)
                real_part = jnp.where(is_first, packed[0], real_part)
                imag_part = jnp.where(is_first, packed[1], imag_part)
            special[index, 0, j] = real_part.astype(BF16)
            special[index, 1, j] = imag_part.astype(BF16)


def pack_row(strided, real_part, imag_part, step):
    half = LANES // 2
    odd = [strided[ri, pl.ds(step // 2, LANES, stride=step), :] for ri in range(2)]
    packed_real = jnp.concatenate([real_part[:half], odd[0][:half]], axis=0)
    packed_imag = jnp.concatenate([imag_part[:half], odd[1][:half]], axis=0)
    top = lax.broadcasted_iota(jnp.int32, packed_imag.shape, 0) == 0
    middle = jnp.broadcast_to(real_part[half : half + 1], packed_imag.shape)
    return packed_real, jnp.where(top, middle, packed_imag)


def pack_kernel(scalars, spec_one, spec_two, special, *refs):
    *outs, strided, turned = refs
    peers = len(outs)
    step = spec_one.shape[2] // LANES
    channels = spec_one.shape[3]
    low_index = scalars[2]
    is_first = scalars[3] == 1
    is_middle = scalars[4] == 1
    row_count = 2 * step
    for index, spec in enumerate((spec_one, spec_two)):
        for a in range(2):
            for ri in range(2):
                strided[ri] = spec[ri, a].astype(F32)
            for low in range(step):
                pair = [strided[ri, pl.ds(low, LANES, stride=step), :] for ri in range(2)]
                if a == 0 and low == 0:
                    packed = pack_row(strided, pair[0], pair[1], step)
                    pair = [jnp.where(is_first, p, v) for p, v in zip(packed, pair)]
                for ri in range(2):
                    value = pair[ri]
                    if a == 0 and low < step // 2:
                        other = special[index, ri, low].astype(F32)
                        value = jnp.where(is_middle, other, value)
                    elif a == 0:
                        j = low - step // 2
                        own = strided[ri, pl.ds(j, LANES, stride=step), :]
                        other = special[index, ri, j].astype(F32)
                        value = jnp.where(is_first, other, jnp.where(is_middle, own, value))
                    row = ri * row_count + a * step + low
                    turned[pl.ds(row, channels, stride=2 * row_count), :] = value.T
        block = channels // peers * 2 * row_count
        for s, out in enumerate(outs):
            start = pl.multiple_of((low_index ^ s) * block, block)
            out[index] = turned[pl.ds(start, block), :].astype(BF16)


def split_value(value):
    high = value.astype(BF16)
    return high, (value - high.astype(F32)).astype(BF16)


def split_columns(value):
    high, low = split_value(value)
    return jnp.concatenate([high, high, low], axis=1)


def split_rows(value):
    high, low = split_value(value)
    return jnp.concatenate([high, high, low], axis=0)


def dot(left, right):
    return jnp.dot(left, right, preferred_element_type=F32)


def conv_kernel(peers, scalars, skip_one, skip_two, data, *refs):
    blocks = refs[:peers]
    (
        forward_one,
        inverse_one,
        cosine_ref,
        sine_ref,
        forward_two,
        inverse_two,
        forward_row,
        inverse_row,
        out,
        filters,
    ) = refs[peers:]
    devices = data.shape[0]
    per_device = data.shape[1] // 2
    rows = cosine_ref.shape[1]
    step = rows // devices
    count = per_device // step
    row_count = 2 * step
    low_index = scalars[2]
    for s in range(peers):
        filters[low_index ^ s] = blocks[s][...].reshape(2, count, 2 * row_count, LANES)
    cosine, sine = cosine_ref[0], sine_ref[0]
    top_row = lax.broadcasted_iota(jnp.int32, (step, 2 * LANES), 0) == 0
    corner = top_row[:, :LANES] & (lax.broadcasted_iota(jnp.int32, (step, LANES), 1) == 0)

    def with_top(values, tops):
        return [
            jnp.concatenate(
                [jnp.where(top_row, tops[c * step : (c + 1) * step], v[:step]), v[step:]], axis=0
            )
            for c, v in enumerate(values)
        ]

    def second_stage(values, table, row_table):
        main = dot(split_columns(jnp.concatenate(values, axis=0)), table[...])
        tops = dot(split_columns(jnp.concatenate([v[:step] for v in values], axis=0)), row_table[...])
        return with_top([main[c * rows : (c + 1) * rows] for c in range(GROUP)], tops)

    def convolve(fields, index, first):
        joined = jnp.concatenate(fields, axis=1)
        staged = dot(forward_one[0], jnp.concatenate([joined, joined], axis=0))
        turned = []
        for c in range(GROUP):
            lanes = slice(c * LANES, (c + 1) * LANES)
            real_part, imag_part = staged[:rows, lanes], staged[rows:, lanes]
            turned.append(
                jnp.concatenate(
                    [
                        real_part * cosine - imag_part * sine,
                        real_part * sine + imag_part * cosine,
                    ],
                    axis=1,
                )
            )
        spectral = second_stage(turned, forward_two, forward_row)
        products = []
        for c in range(GROUP):
            stored = filters[:, index, first + c]
            h_real = stored[:, :row_count].reshape(rows, LANES).astype(F32)
            h_imag = stored[:, row_count:].reshape(rows, LANES).astype(F32)
            x_real, x_imag = spectral[c][:, :LANES], spectral[c][:, LANES:]
            real_real, imag_imag = x_real * h_real, x_imag * h_imag
            y_real = real_real - imag_imag
            y_imag = x_real * h_imag + x_imag * h_real
            y_real = jnp.concatenate(
                [jnp.where(corner, real_real[:step], y_real[:step]), y_real[step:]], axis=0
            )
            y_imag = jnp.concatenate(
                [jnp.where(corner, imag_imag[:step], y_imag[:step]), y_imag[step:]], axis=0
            )
            products.append(jnp.concatenate([y_real, y_imag], axis=1))
        inverted = second_stage(products, inverse_two, inverse_row)
        columns = []
        for c in range(GROUP):
            real_part, imag_part = inverted[c][:, :LANES], inverted[c][:, LANES:]
            columns.append(
                jnp.concatenate(
                    [
                        real_part * cosine + imag_part * sine,
                        imag_part * cosine - real_part * sine,
                    ],
                    axis=0,
                )
            )
        result = dot(inverse_one[0], split_rows(jnp.concatenate(columns, axis=1)))
        return [result[:, c * LANES : (c + 1) * LANES] for c in range(GROUP)]

    def body(trip, carry):
        first = trip * GROUP
        size = GROUP * step
        base = pl.multiple_of(first * step, size)
        signal_rows = data[:, pl.ds(base, size), :].astype(F32)
        gate_rows = data[:, pl.ds(pl.multiple_of(per_device + base, size), size), :].astype(F32)

        def channel(values, c):
            return values[:, c * step : (c + 1) * step, :].reshape(rows, LANES)

        fields = [channel(signal_rows, c) for c in range(GROUP)]
        results = convolve([f.astype(BF16) for f in fields], 0, first)
        skip_base = scalars[0] * count + first
        middles = [
            (channel(gate_rows, c) * (results[c] + skip_one[skip_base + c] * fields[c])).astype(BF16)
            for c in range(GROUP)
        ]
        results = convolve(middles, 1, first)
        finals = [
            (results[c] + skip_two[skip_base + c] * middles[c].astype(F32)).reshape(
                devices, step, LANES
            )
            for c in range(GROUP)
        ]
        out[:, pl.ds(base, size), :] = jnp.concatenate(finals, axis=1).astype(BF16)
        return carry

    lax.fori_loop(0, count // GROUP, body, 0)


def final_kernel(back, gate, out, turned):
    step = gate.shape[0] // LANES
    channels = gate.shape[1]
    turned[...] = back[...].astype(F32).reshape(channels * step, LANES)
    for t in range(step):
        piece = pl.ds(t * LANES, LANES)
        value = turned[pl.ds(t, channels, stride=step), :].T
        out[piece, :] = (gate[piece, :].astype(F32) * value).astype(BF16)


def whole(shape):
    zeros = (0,) * len(shape)
    return pl.BlockSpec(shape, lambda i, scalars: zeros)


def by_half(shape):
    zeros = (0,) * (len(shape) - 1)
    return pl.BlockSpec((1,) + tuple(shape[1:]), lambda i, scalars: (scalars[1],) + zeros)


def on_device(signal, gate_one, mix_two, gate_two, skip_one, skip_two, spectrum_one, spectrum_two):
    n = lax.axis_size("ctx")
    me = lax.axis_index("ctx")
    peers = n // 2
    length, channels = signal.shape
    step = length // LANES
    count = channels // n
    per_device = count * step
    half_channels = channels // 2
    scalars = jnp.stack(
        [me, me // peers, me % peers, (me == 0).astype(jnp.int32), (me == peers).astype(jnp.int32)]
    ).astype(jnp.int32)

    other_half = pl.BlockSpec((2, 1, length, half_channels), lambda i, s: (0, 0, 0, 1 - s[1]))
    data, special = pl.pallas_call(
        prep_kernel,
        grid_spec=pltpu.PrefetchScalarGridSpec(
            num_scalar_prefetch=1,
            grid=(1,),
            in_specs=[whole(signal.shape)] * 3 + [other_half] * 2,
            out_specs=[
                whole((n, 2 * per_device, LANES)),
                whole((2, 2, step // 2, LANES, half_channels)),
            ],
            scratch_shapes=[
                pltpu.VMEM((channels * step, LANES), F32),
                pltpu.VMEM((2, length, half_channels), F32),
            ],
        ),
        out_shape=[
            jax.ShapeDtypeStruct((n, 2 * per_device, LANES), BF16),
            jax.ShapeDtypeStruct((2, 2, step // 2, LANES, half_channels), BF16),
        ],
        compiler_params=PARAMS,
        name="prep",
    )(scalars, signal, gate_one, mix_two, spectrum_one, spectrum_two)
    special = lax.ppermute(special, "ctx", [(0, peers), (peers, 0)])
    data = lax.all_to_all(data, "ctx", split_axis=0, concat_axis=0, tiled=True)

    block_shape = (2, count * 4 * step, LANES)
    own_half = pl.BlockSpec((2, 2, length, half_channels), lambda i, s: (0, 0, 0, s[1]))
    blocks = pl.pallas_call(
        pack_kernel,
        grid_spec=pltpu.PrefetchScalarGridSpec(
            num_scalar_prefetch=1,
            grid=(1,),
            in_specs=[own_half] * 2 + [whole(special.shape)],
            out_specs=[whole(block_shape)] * peers,
            scratch_shapes=[
                pltpu.VMEM((2, length, half_channels), F32),
                pltpu.VMEM((half_channels * 4 * step, LANES), F32),
            ],
        ),
        out_shape=[jax.ShapeDtypeStruct(block_shape, BF16)] * peers,
        compiler_params=PARAMS,
        name="pack",
    )(scalars, spectrum_one, spectrum_two, special)
    blocks = [
        block if s == 0 else lax.ppermute(block, "ctx", [(i, i ^ s) for i in range(n)])
        for s, block in enumerate(blocks)
    ]

    tables = {name: jnp.asarray(table) for name, table in make_tables(n, step).items()}
    out = pl.pallas_call(
        functools.partial(conv_kernel, peers),
        grid_spec=pltpu.PrefetchScalarGridSpec(
            num_scalar_prefetch=1,
            grid=(1,),
            in_specs=[pl.BlockSpec(memory_space=pltpu.SMEM)] * 2
            + [whole(data.shape)]
            + [whole(block_shape)] * peers
            + [by_half(tables[name].shape) for name in ("forward_one", "inverse_one", "cosine", "sine")]
            + [whole((3 * 2 * LANES, 2 * LANES))] * 4,
            out_specs=whole((n, per_device, LANES)),
            scratch_shapes=[pltpu.VMEM((peers, 2, count, 4 * step, LANES), BF16)],
        ),
        out_shape=jax.ShapeDtypeStruct((n, per_device, LANES), BF16),
        compiler_params=PARAMS,
        name="convolve",
    )(scalars, skip_one, skip_two, data, *blocks, *tables.values())

    back = lax.all_to_all(out, "ctx", split_axis=0, concat_axis=0, tiled=True)
    return pl.pallas_call(
        final_kernel,
        out_shape=jax.ShapeDtypeStruct((length, channels), BF16),
        scratch_shapes=[pltpu.VMEM((channels * step, LANES), F32)],
        compiler_params=PARAMS,
        name="final",
    )(back, gate_two)


def solution(mesh):
    return jax.shard_map(
        on_device,
        mesh=mesh,
        in_specs=(
            P(("group", "ctx"), None),
            P(("group", "ctx"), None),
            P(("group", "ctx"), None),
            P(("group", "ctx"), None),
            P(),
            P(),
            P(None, "ctx", None, None),
            P(None, "ctx", None, None),
        ),
        out_specs=P(("group", "ctx"), None),
        check_vma=False,
    )
```

```python
import functools

import jax
import jax.numpy as jnp
import numpy as np
from jax import lax
from jax.experimental import pallas as pl
from jax.experimental.pallas import tpu as pltpu
from jax.sharding import PartitionSpec as P

F32 = jnp.float32
BF16 = jnp.bfloat16
LANES = 128
GROUP = 4
PARAMS = pltpu.CompilerParams(vmem_limit_bytes=60 * 1024 * 1024)


def split_table(table):
    high = table.astype(jnp.bfloat16)
    low = (table - high.astype(np.float64)).astype(jnp.bfloat16)
    return high, low


def make_tables(n, step):
    rows = n * step
    first_len = 2 * rows
    total = first_len * LANES
    turn = 2.0 * np.pi
    n1 = np.arange(rows)
    n2 = np.arange(LANES)
    forward_one, inverse_one, cosines, sines = [], [], [], []
    for half in range(2):
        k1 = np.array(
            [
                2 * (half * (n // 2) + source) + a + 2 * n * low
                for source in range(n // 2)
                for a in range(2)
                for low in range(step)
            ]
        )
        k1[:step] = [2 * n * j for j in range(step // 2)] + [n + 2 * n * j for j in range(step // 2)]
        angle = turn * ((k1[:, None] * n1[None, :]) % first_len) / first_len
        real_rows, imag_rows = np.cos(angle), -np.sin(angle)
        imag_rows[0] = np.cos(np.pi * n1)
        table = np.concatenate([real_rows, imag_rows], axis=0)
        forward_one.append(table)
        weight = np.full((2 * rows, 1), 2.0 / total)
        weight[0] = weight[rows] = 1.0 / total
        inverse_one.append((table * weight).T)
        angle = turn * ((k1[:, None] * n2[None, :]) % total) / total
        angle[0] = 0.0
        cosines.append(np.cos(angle))
        sines.append(-np.sin(angle))
    angle = turn * ((n2[:, None] * n2[None, :]) % LANES) / LANES
    cosine, sine = np.cos(angle), np.sin(angle)
    forward_two = np.block([[cosine, -sine], [sine, cosine]])
    inverse_two = np.block([[cosine, sine], [-sine, cosine]])
    half_lanes = LANES // 2
    even = turn * ((n2[:, None] * np.arange(half_lanes)[None, :]) % LANES) / LANES
    odd = turn * ((n2[:, None] * (1 + 2 * np.arange(half_lanes))[None, :]) % (2 * LANES)) / (2 * LANES)
    zero = np.zeros((LANES, half_lanes))
    even_imag = -np.sin(even)
    even_imag[:, 0] = np.cos(np.pi * n2)
    forward_row = np.block(
        [[np.cos(even), zero, even_imag, zero], [zero, np.cos(odd), zero, -np.sin(odd)]]
    )
    weight = np.full((2 * LANES, 1), 2.0)
    weight[0] = weight[LANES] = 1.0
    inverse_row = (forward_row * weight[:, 0][None, :]).T

    def along_rows(table):
        high, low = split_table(table)
        return np.concatenate([high, low, high], axis=0)

    def along_columns(table):
        high, low = split_table(table)
        return np.concatenate([high, low, high], axis=1)

    def two_columns(table):
        return np.concatenate(split_table(table), axis=1)

    return {
        "forward_one": np.stack([two_columns(t) for t in forward_one]),
        "inverse_one": np.stack([along_columns(t) for t in inverse_one]),
        "cosine": np.stack(cosines).astype(np.float32),
        "sine": np.stack(sines).astype(np.float32),
        "forward_two": along_rows(forward_two),
        "inverse_two": along_rows(inverse_two),
        "forward_row": along_rows(forward_row),
        "inverse_row": along_rows(inverse_row),
    }


def prep_kernel(signal, gate, mix, data, turned):
    step = signal.shape[0] // LANES
    channels = signal.shape[1]
    devices = data.shape[0]
    rows = data.shape[1] // 2
    for part in range(2):
        for t in range(step):
            piece = pl.ds(t * LANES, LANES)
            if part == 0:
                value = signal[piece, :].astype(F32)
            else:
                value = gate[piece, :].astype(F32) * mix[piece, :].astype(F32)
            turned[pl.ds(t, channels, stride=step), :] = value.T
        data[:, part * rows : (part + 1) * rows, :] = (
            turned[...].reshape(devices, rows, LANES).astype(BF16)
        )


def special_kernel(scalars, spec_one, spec_two, special, strided):
    step = spec_one.shape[2] // LANES
    is_first = scalars[3] == 1
    for index, spec in enumerate((spec_one, spec_two)):
        for ri in range(2):
            strided[ri] = spec[ri, 0].astype(F32)
        for j in range(step // 2):
            real_part, imag_part = (
                strided[ri, pl.ds(j, LANES, stride=step), :] for ri in range(2)
            )
            if j == 0:
                packed = pack_row(strided, real_part, imag_part, step)
                real_part = jnp.where(is_first, packed[0], real_part)
                imag_part = jnp.where(is_first, packed[1], imag_part)
            special[index, 0, j] = real_part.astype(BF16)
            special[index, 1, j] = imag_part.astype(BF16)


def pack_row(strided, real_part, imag_part, step):
    half = LANES // 2
    odd = [strided[ri, pl.ds(step // 2, LANES, stride=step), :] for ri in range(2)]
    packed_real = jnp.concatenate([real_part[:half], odd[0][:half]], axis=0)
    packed_imag = jnp.concatenate([imag_part[:half], odd[1][:half]], axis=0)
    top = lax.broadcasted_iota(jnp.int32, packed_imag.shape, 0) == 0
    middle = jnp.broadcast_to(real_part[half : half + 1], packed_imag.shape)
    return packed_real, jnp.where(top, middle, packed_imag)


def pack_kernel(scalars, spec_one, spec_two, special, *refs):
    *outs, strided, turned = refs
    peers = len(outs)
    step = spec_one.shape[2] // LANES
    channels = spec_one.shape[3]
    low_index = scalars[2]
    is_first = scalars[3] == 1
    is_middle = scalars[4] == 1
    row_count = 2 * step
    for index, spec in enumerate((spec_one, spec_two)):
        for a in range(2):
            for ri in range(2):
                strided[ri] = spec[ri, a].astype(F32)
            for low in range(step):
                pair = [strided[ri, pl.ds(low, LANES, stride=step), :] for ri in range(2)]
                if a == 0 and low == 0:
                    packed = pack_row(strided, pair[0], pair[1], step)
                    pair = [jnp.where(is_first, p, v) for p, v in zip(packed, pair)]
                for ri in range(2):
                    value = pair[ri]
                    if a == 0 and low < step // 2:
                        other = special[index, ri, low].astype(F32)
                        value = jnp.where(is_middle, other, value)
                    elif a == 0:
                        j = low - step // 2
                        own = strided[ri, pl.ds(j, LANES, stride=step), :]
                        other = special[index, ri, j].astype(F32)
                        value = jnp.where(is_first, other, jnp.where(is_middle, own, value))
                    row = ri * row_count + a * step + low
                    turned[pl.ds(row, channels, stride=2 * row_count), :] = value.T
        block = channels // peers * 2 * row_count
        for s, out in enumerate(outs):
            start = pl.multiple_of((low_index ^ s) * block, block)
            out[index] = turned[pl.ds(start, block), :].astype(BF16)


def split_value(value):
    high = value.astype(BF16)
    return high, (value - high.astype(F32)).astype(BF16)


def split_columns(value):
    high, low = split_value(value)
    return jnp.concatenate([high, high, low], axis=1)


def split_rows(value):
    high, low = split_value(value)
    return jnp.concatenate([high, high, low], axis=0)


def dot(left, right):
    return jnp.dot(left, right, preferred_element_type=F32)


def conv_kernel(peers, scalars, skip_one, skip_two, data, *refs):
    blocks = refs[:peers]
    (
        forward_one,
        inverse_one,
        cosine_ref,
        sine_ref,
        forward_two,
        inverse_two,
        forward_row,
        inverse_row,
        out,
        filters,
        landed,
    ) = refs[peers:]
    devices = data.shape[0]
    per_device = data.shape[1] // 2
    rows = cosine_ref.shape[1]
    step = rows // devices
    count = per_device // step
    row_count = 2 * step
    low_index = scalars[2]
    copies = [
        pltpu.make_async_copy(blocks[s], filters.at[low_index ^ s], landed.at[s])
        for s in range(peers)
    ]
    for copy in copies:
        copy.start()
    for copy in copies:
        copy.wait()
    cosine, sine = cosine_ref[0], sine_ref[0]
    top_row = lax.broadcasted_iota(jnp.int32, (step, 2 * LANES), 0) == 0
    corner = top_row[:, :LANES] & (lax.broadcasted_iota(jnp.int32, (step, LANES), 1) == 0)

    def with_top(values, tops):
        return [
            jnp.concatenate(
                [jnp.where(top_row, tops[c * step : (c + 1) * step], v[:step]), v[step:]], axis=0
            )
            for c, v in enumerate(values)
        ]

    def second_stage(values, table, row_table):
        main = dot(split_columns(jnp.concatenate(values, axis=0)), table[...])
        tops = dot(split_columns(jnp.concatenate([v[:step] for v in values], axis=0)), row_table[...])
        return with_top([main[c * rows : (c + 1) * rows] for c in range(GROUP)], tops)

    def convolve(fields, index, first):
        joined = jnp.concatenate(fields, axis=1)
        staged = dot(forward_one[0], jnp.concatenate([joined, joined], axis=0))
        turned = []
        for c in range(GROUP):
            lanes = slice(c * LANES, (c + 1) * LANES)
            real_part, imag_part = staged[:rows, lanes], staged[rows:, lanes]
            turned.append(
                jnp.concatenate(
                    [
                        real_part * cosine - imag_part * sine,
                        real_part * sine + imag_part * cosine,
                    ],
                    axis=1,
                )
            )
        spectral = second_stage(turned, forward_two, forward_row)
        products = []
        for c in range(GROUP):
            stored = filters[:, index, pl.ds(pl.multiple_of((first + c) * 2 * row_count, 2 * row_count), 2 * row_count), :]
            h_real = stored[:, :row_count].reshape(rows, LANES).astype(F32)
            h_imag = stored[:, row_count:].reshape(rows, LANES).astype(F32)
            x_real, x_imag = spectral[c][:, :LANES], spectral[c][:, LANES:]
            real_real, imag_imag = x_real * h_real, x_imag * h_imag
            y_real = real_real - imag_imag
            y_imag = x_real * h_imag + x_imag * h_real
            y_real = jnp.concatenate(
                [jnp.where(corner, real_real[:step], y_real[:step]), y_real[step:]], axis=0
            )
            y_imag = jnp.concatenate(
                [jnp.where(corner, imag_imag[:step], y_imag[:step]), y_imag[step:]], axis=0
            )
            products.append(jnp.concatenate([y_real, y_imag], axis=1))
        inverted = second_stage(products, inverse_two, inverse_row)
        columns = []
        for c in range(GROUP):
            real_part, imag_part = inverted[c][:, :LANES], inverted[c][:, LANES:]
            columns.append(
                jnp.concatenate(
                    [
                        real_part * cosine + imag_part * sine,
                        imag_part * cosine - real_part * sine,
                    ],
                    axis=0,
                )
            )
        result = dot(inverse_one[0], split_rows(jnp.concatenate(columns, axis=1)))
        return [result[:, c * LANES : (c + 1) * LANES] for c in range(GROUP)]

    def body(trip, carry):
        first = trip * GROUP
        size = GROUP * step
        base = pl.multiple_of(first * step, size)
        signal_rows = data[:, pl.ds(base, size), :].astype(F32)
        gate_rows = data[:, pl.ds(pl.multiple_of(per_device + base, size), size), :].astype(F32)

        def channel(values, c):
            return values[:, c * step : (c + 1) * step, :].reshape(rows, LANES)

        fields = [channel(signal_rows, c) for c in range(GROUP)]
        results = convolve([f.astype(BF16) for f in fields], 0, first)
        skip_base = scalars[0] * count + first
        middles = [
            (channel(gate_rows, c) * (results[c] + skip_one[skip_base + c] * fields[c])).astype(BF16)
            for c in range(GROUP)
        ]
        results = convolve(middles, 1, first)
        finals = [
            (results[c] + skip_two[skip_base + c] * middles[c].astype(F32)).reshape(
                devices, step, LANES
            )
            for c in range(GROUP)
        ]
        out[:, pl.ds(base, size), :] = jnp.concatenate(finals, axis=1).astype(BF16)
        return carry

    lax.fori_loop(0, count // GROUP, body, 0)


def final_kernel(back, gate, out, turned):
    step = gate.shape[0] // LANES
    channels = gate.shape[1]
    turned[...] = back[...].astype(F32).reshape(channels * step, LANES)
    for t in range(step):
        piece = pl.ds(t * LANES, LANES)
        value = turned[pl.ds(t, channels, stride=step), :].T
        out[piece, :] = (gate[piece, :].astype(F32) * value).astype(BF16)


def whole(shape):
    zeros = (0,) * len(shape)
    return pl.BlockSpec(shape, lambda i, scalars: zeros)


def by_half(shape):
    zeros = (0,) * (len(shape) - 1)
    return pl.BlockSpec((1,) + tuple(shape[1:]), lambda i, scalars: (scalars[1],) + zeros)


def on_device(signal, gate_one, mix_two, gate_two, skip_one, skip_two, spectrum_one, spectrum_two):
    n = lax.axis_size("ctx")
    me = lax.axis_index("ctx")
    peers = n // 2
    length, channels = signal.shape
    step = length // LANES
    count = channels // n
    per_device = count * step
    half_channels = channels // 2
    scalars = jnp.stack(
        [me, me // peers, me % peers, (me == 0).astype(jnp.int32), (me == peers).astype(jnp.int32)]
    ).astype(jnp.int32)

    other_half = pl.BlockSpec((2, 1, length, half_channels), lambda i, s: (0, 0, 0, 1 - s[1]))
    special = pl.pallas_call(
        special_kernel,
        grid_spec=pltpu.PrefetchScalarGridSpec(
            num_scalar_prefetch=1,
            grid=(1,),
            in_specs=[other_half] * 2,
            out_specs=whole((2, 2, step // 2, LANES, half_channels)),
            scratch_shapes=[pltpu.VMEM((2, length, half_channels), F32)],
        ),
        out_shape=jax.ShapeDtypeStruct((2, 2, step // 2, LANES, half_channels), BF16),
        compiler_params=PARAMS,
        name="special",
    )(scalars, spectrum_one, spectrum_two)
    special = lax.ppermute(special, "ctx", [(0, peers), (peers, 0)])
    data = pl.pallas_call(
        prep_kernel,
        out_shape=jax.ShapeDtypeStruct((n, 2 * per_device, LANES), BF16),
        scratch_shapes=[pltpu.VMEM((channels * step, LANES), F32)],
        compiler_params=PARAMS,
        name="prep",
    )(signal, gate_one, mix_two)
    data, special = lax.optimization_barrier((data, special))
    data = lax.all_to_all(data, "ctx", split_axis=0, concat_axis=0, tiled=True)

    block_shape = (2, count * 4 * step, LANES)
    own_half = pl.BlockSpec((2, 2, length, half_channels), lambda i, s: (0, 0, 0, s[1]))
    blocks = pl.pallas_call(
        pack_kernel,
        grid_spec=pltpu.PrefetchScalarGridSpec(
            num_scalar_prefetch=1,
            grid=(1,),
            in_specs=[own_half] * 2 + [whole(special.shape)],
            out_specs=[whole(block_shape)] * peers,
            scratch_shapes=[
                pltpu.VMEM((2, length, half_channels), F32),
                pltpu.VMEM((half_channels * 4 * step, LANES), F32),
            ],
        ),
        out_shape=[jax.ShapeDtypeStruct(block_shape, BF16)] * peers,
        compiler_params=PARAMS,
        name="pack",
    )(scalars, spectrum_one, spectrum_two, special)
    blocks = [
        block if s == 0 else lax.ppermute(block, "ctx", [(i, i ^ s) for i in range(n)])
        for s, block in enumerate(blocks)
    ]

    tables = {name: jnp.asarray(table) for name, table in make_tables(n, step).items()}
    out = pl.pallas_call(
        functools.partial(conv_kernel, peers),
        grid_spec=pltpu.PrefetchScalarGridSpec(
            num_scalar_prefetch=1,
            grid=(1,),
            in_specs=[pl.BlockSpec(memory_space=pltpu.SMEM)] * 2
            + [whole(data.shape)]
            + [pl.BlockSpec(memory_space=pl.ANY)] * peers
            + [by_half(tables[name].shape) for name in ("forward_one", "inverse_one", "cosine", "sine")]
            + [whole((3 * 2 * LANES, 2 * LANES))] * 4,
            out_specs=whole((n, per_device, LANES)),
            scratch_shapes=[
                pltpu.VMEM((peers,) + block_shape, BF16),
                pltpu.SemaphoreType.DMA((peers,)),
            ],
        ),
        out_shape=jax.ShapeDtypeStruct((n, per_device, LANES), BF16),
        compiler_params=PARAMS,
        name="convolve",
    )(scalars, skip_one, skip_two, data, *blocks, *tables.values())

    back = lax.all_to_all(out, "ctx", split_axis=0, concat_axis=0, tiled=True)
    return pl.pallas_call(
        final_kernel,
        out_shape=jax.ShapeDtypeStruct((length, channels), BF16),
        scratch_shapes=[pltpu.VMEM((channels * step, LANES), F32)],
        compiler_params=PARAMS,
        name="final",
    )(back, gate_two)


def solution(mesh):
    return jax.shard_map(
        on_device,
        mesh=mesh,
        in_specs=(
            P(("group", "ctx"), None),
            P(("group", "ctx"), None),
            P(("group", "ctx"), None),
            P(("group", "ctx"), None),
            P(),
            P(),
            P(None, "ctx", None, None),
            P(None, "ctx", None, None),
        ),
        out_specs=P(("group", "ctx"), None),
        check_vma=False,
    )
```

```python
import functools

import jax
import jax.numpy as jnp
import numpy as np
from jax import lax
from jax.experimental import pallas as pl
from jax.experimental.pallas import tpu as pltpu
from jax.sharding import PartitionSpec as P

F32 = jnp.float32
BF16 = jnp.bfloat16
LANES = 128
GROUP = 8
SMALL = pltpu.CompilerParams(vmem_limit_bytes=24 * 1024 * 1024)
PARAMS = pltpu.CompilerParams(vmem_limit_bytes=60 * 1024 * 1024)


def split_table(table):
    high = table.astype(jnp.bfloat16)
    low = (table - high.astype(np.float64)).astype(jnp.bfloat16)
    return high, low


def make_tables(n, step):
    rows = n * step
    first_len = 2 * rows
    total = first_len * LANES
    turn = 2.0 * np.pi
    n1 = np.arange(rows)
    n2 = np.arange(LANES)
    forward_one, inverse_one, cosines, sines = [], [], [], []
    for half in range(2):
        k1 = np.array(
            [
                2 * (half * (n // 2) + source) + a + 2 * n * low
                for source in range(n // 2)
                for a in range(2)
                for low in range(step)
            ]
        )
        k1[:step] = [2 * n * j for j in range(step // 2)] + [n + 2 * n * j for j in range(step // 2)]
        angle = turn * ((k1[:, None] * n1[None, :]) % first_len) / first_len
        real_rows, imag_rows = np.cos(angle), -np.sin(angle)
        imag_rows[0] = np.cos(np.pi * n1)
        table = np.concatenate([real_rows, imag_rows], axis=0)
        forward_one.append(table)
        weight = np.full((2 * rows, 1), 2.0 / total)
        weight[0] = weight[rows] = 1.0 / total
        inverse_one.append((table * weight).T)
        angle = turn * ((k1[:, None] * n2[None, :]) % total) / total
        angle[0] = 0.0
        cosines.append(np.cos(angle))
        sines.append(-np.sin(angle))
    angle = turn * ((n2[:, None] * n2[None, :]) % LANES) / LANES
    cosine, sine = np.cos(angle), np.sin(angle)
    forward_two = np.block([[cosine, -sine], [sine, cosine]])
    inverse_two = np.block([[cosine, sine], [-sine, cosine]])
    half_lanes = LANES // 2
    even = turn * ((n2[:, None] * np.arange(half_lanes)[None, :]) % LANES) / LANES
    odd = turn * ((n2[:, None] * (1 + 2 * np.arange(half_lanes))[None, :]) % (2 * LANES)) / (2 * LANES)
    zero = np.zeros((LANES, half_lanes))
    even_imag = -np.sin(even)
    even_imag[:, 0] = np.cos(np.pi * n2)
    forward_row = np.block(
        [[np.cos(even), zero, even_imag, zero], [zero, np.cos(odd), zero, -np.sin(odd)]]
    )
    weight = np.full((2 * LANES, 1), 2.0)
    weight[0] = weight[LANES] = 1.0
    inverse_row = (forward_row * weight[:, 0][None, :]).T

    def along_rows(table):
        high, low = split_table(table)
        return np.concatenate([high, low, high], axis=0)

    def along_columns(table):
        high, low = split_table(table)
        return np.concatenate([high, low, high], axis=1)

    def two_columns(table):
        return np.concatenate(split_table(table), axis=1)

    return {
        "forward_one": np.stack([two_columns(t) for t in forward_one]),
        "inverse_one": np.stack([along_columns(t) for t in inverse_one]),
        "turns": np.stack([cosines, sines], axis=1).astype(np.float32),
        "forward_two": along_rows(forward_two),
        "inverse_two": along_rows(inverse_two),
        "forward_row": along_rows(forward_row),
        "inverse_row": along_rows(inverse_row),
    }


def prep_kernel(signal, gate, mix, data, turned):
    step = signal.shape[0] // LANES
    channels = signal.shape[1]
    devices = data.shape[0]
    rows = data.shape[1] // 2
    for part in range(2):
        for t in range(step):
            piece = pl.ds(t * LANES, LANES)
            if part == 0:
                value = signal[piece, :].astype(F32)
            else:
                value = gate[piece, :].astype(F32) * mix[piece, :].astype(F32)
            turned[pl.ds(t, channels, stride=step), :] = value.T
        data[:, part * rows : (part + 1) * rows, :] = (
            turned[...].reshape(devices, rows, LANES).astype(BF16)
        )


def place():
    n = lax.axis_size("ctx")
    me = lax.axis_index("ctx")
    peers = n // 2
    return me, me // peers, lax.rem(me, peers), me == 0, me == peers


def special_kernel(spec_one, spec_two, special, raw, strided, landed):
    step = spec_one.shape[2] // LANES
    width = raw.shape[3]
    _, half, _, is_first, _ = place()
    columns = pl.ds(pl.multiple_of((1 - half) * width, width), width)
    copies = [
        pltpu.make_async_copy(spec.at[ri, 0, :, columns], raw.at[index, ri], landed.at[index, ri])
        for index, spec in enumerate((spec_one, spec_two))
        for ri in range(2)
    ]
    for copy in copies:
        copy.start()
    for index in range(2):
        for ri in range(2):
            copies[2 * index + ri].wait()
            strided[ri] = raw[index, ri].astype(F32)
        for j in range(step // 2):
            pair = [strided[ri, pl.ds(j, LANES, stride=step), :] for ri in range(2)]
            if j == 0:
                packed = pack_row(strided, pair[0], pair[1], step)
                pair = [jnp.where(is_first, p, v) for p, v in zip(packed, pair)]
            for ri in range(2):
                special[index, ri, j] = pair[ri].astype(BF16)


def pack_row(strided, real_part, imag_part, step):
    half = LANES // 2
    odd = [strided[ri, pl.ds(step // 2, LANES, stride=step), :] for ri in range(2)]
    packed_real = jnp.concatenate([real_part[:half], odd[0][:half]], axis=0)
    packed_imag = jnp.concatenate([imag_part[:half], odd[1][:half]], axis=0)
    top = lax.broadcasted_iota(jnp.int32, packed_imag.shape, 0) == 0
    middle = jnp.broadcast_to(real_part[half : half + 1], packed_imag.shape)
    return packed_real, jnp.where(top, middle, packed_imag)


def pack_kernel(index, spec, special, *refs):
    *outs, raw, strided, turned, landed = refs
    peers = len(outs)
    step = spec.shape[2] // LANES
    channels = raw.shape[3]
    _, half, low_index, is_first, is_middle = place()
    row_count = 2 * step
    columns = pl.ds(pl.multiple_of(half * channels, channels), channels)
    copies = {
        (a, ri): pltpu.make_async_copy(
            spec.at[ri, a, :, columns], raw.at[a, ri], landed.at[a, ri]
        )
        for a in (1, 0)
        for ri in range(2)
    }
    for copy in copies.values():
        copy.start()
    for a in (1, 0):
        for ri in range(2):
            copies[a, ri].wait()
            strided[ri] = raw[a, ri].astype(F32)
        for low in range(step):
            pair = [strided[ri, pl.ds(low, LANES, stride=step), :] for ri in range(2)]
            if a == 0 and low == 0:
                packed = pack_row(strided, pair[0], pair[1], step)
                pair = [jnp.where(is_first, p, v) for p, v in zip(packed, pair)]
            for ri in range(2):
                value = pair[ri]
                if a == 0 and low < step // 2:
                    other = special[index, ri, low].astype(F32)
                    value = jnp.where(is_middle, other, value)
                elif a == 0:
                    j = low - step // 2
                    own = strided[ri, pl.ds(j, LANES, stride=step), :]
                    other = special[index, ri, j].astype(F32)
                    value = jnp.where(is_first, other, jnp.where(is_middle, own, value))
                row = ri * row_count + a * step + low
                turned[pl.ds(row, channels, stride=2 * row_count), :] = value.T
    block = channels // peers * 2 * row_count
    for s, out in enumerate(outs):
        start = pl.multiple_of((low_index ^ s) * block, block)
        out[...] = turned[pl.ds(start, block), :].astype(BF16)


def split_value(value):
    high = value.astype(BF16)
    return high, (value - high.astype(F32)).astype(BF16)


def split_columns(value):
    high, low = split_value(value)
    return jnp.concatenate([high, high, low], axis=1)


def split_rows(value):
    high, low = split_value(value)
    return jnp.concatenate([high, high, low], axis=0)


def dot(left, right):
    return jnp.dot(left, right, preferred_element_type=F32)


HALVED = ("forward_one", "turns", "inverse_one")
PARTS = ("data", "forward_one", "turns", "forward_two", "forward_row")
LATER = ("inverse_two", "inverse_row", "inverse_one")


def conv_kernel(peers, gated, skip, *refs):
    names = PARTS + LATER
    sources = dict(zip(names, refs))
    blocks, refs = refs[len(names) : len(names) + peers], refs[len(names) + peers :]
    out, refs = refs[0], refs[1:]
    buffers = dict(zip(names, refs))
    filters, landed = refs[len(names) :]
    me, half, low_index, _, _ = place()
    copies = {}
    for i, name in enumerate(names):
        source = sources[name].at[half] if name in HALVED else sources[name]
        copies[name] = pltpu.make_async_copy(source, buffers[name], landed.at[i])
    for s in range(peers):
        copies[s] = pltpu.make_async_copy(
            blocks[s], filters.at[low_index ^ s], landed.at[len(names) + s]
        )
    for name in PARTS + tuple(range(peers)) + LATER:
        copies[name].start()
    awaited = set()

    def need(*wanted):
        for name in wanted:
            if name not in awaited:
                awaited.add(name)
                copies[name].wait()

    data, turns = buffers["data"], buffers["turns"]
    devices = data.shape[0]
    per_device = out.shape[1]
    rows = turns.shape[1]
    step = rows // devices
    count = per_device // step
    row_count = 2 * step
    top_row = lax.broadcasted_iota(jnp.int32, (step, 2 * LANES), 0) == 0
    corner = top_row[:, :LANES] & (lax.broadcasted_iota(jnp.int32, (step, LANES), 1) == 0)

    def with_top(values, tops):
        return [
            jnp.concatenate(
                [jnp.where(top_row, tops[c * step : (c + 1) * step], v[:step]), v[step:]], axis=0
            )
            for c, v in enumerate(values)
        ]

    def second_stage(values, table, row_table):
        need(table, row_table)
        main = dot(split_columns(jnp.concatenate(values, axis=0)), buffers[table][...])
        tops = dot(split_columns(jnp.concatenate([v[:step] for v in values], axis=0)), buffers[row_table][...])
        return with_top([main[c * rows : (c + 1) * rows] for c in range(GROUP)], tops)

    def convolve(fields, first):
        joined = jnp.concatenate(fields, axis=1)
        need("forward_one", "turns")
        cosine, sine = turns[0], turns[1]
        staged = dot(buffers["forward_one"][...], jnp.concatenate([joined, joined], axis=0))
        turned = []
        for c in range(GROUP):
            lanes = slice(c * LANES, (c + 1) * LANES)
            real_part, imag_part = staged[:rows, lanes], staged[rows:, lanes]
            turned.append(
                jnp.concatenate(
                    [
                        real_part * cosine - imag_part * sine,
                        real_part * sine + imag_part * cosine,
                    ],
                    axis=1,
                )
            )
        spectral = second_stage(turned, "forward_two", "forward_row")
        need(*range(peers))
        products = []
        for c in range(GROUP):
            stored = filters[:, pl.ds(pl.multiple_of((first + c) * 2 * row_count, 2 * row_count), 2 * row_count), :]
            h_real = stored[:, :row_count].reshape(rows, LANES).astype(F32)
            h_imag = stored[:, row_count:].reshape(rows, LANES).astype(F32)
            x_real, x_imag = spectral[c][:, :LANES], spectral[c][:, LANES:]
            real_real, imag_imag = x_real * h_real, x_imag * h_imag
            y_real = real_real - imag_imag
            y_imag = x_real * h_imag + x_imag * h_real
            y_real = jnp.concatenate(
                [jnp.where(corner, real_real[:step], y_real[:step]), y_real[step:]], axis=0
            )
            y_imag = jnp.concatenate(
                [jnp.where(corner, imag_imag[:step], y_imag[:step]), y_imag[step:]], axis=0
            )
            products.append(jnp.concatenate([y_real, y_imag], axis=1))
        inverted = second_stage(products, "inverse_two", "inverse_row")
        columns = []
        for c in range(GROUP):
            real_part, imag_part = inverted[c][:, :LANES], inverted[c][:, LANES:]
            columns.append(
                jnp.concatenate(
                    [
                        real_part * cosine + imag_part * sine,
                        imag_part * cosine - real_part * sine,
                    ],
                    axis=0,
                )
            )
        need("inverse_one")
        result = dot(buffers["inverse_one"][...], split_rows(jnp.concatenate(columns, axis=1)))
        return [result[:, c * LANES : (c + 1) * LANES] for c in range(GROUP)]

    need("data")
    size = GROUP * step
    for first in range(0, count, GROUP):

        def channels(start):
            values = data[:, start : start + size, :].astype(F32)
            return [
                values[:, c * step : (c + 1) * step, :].reshape(rows, LANES) for c in range(GROUP)
            ]

        base = first * step
        fields = channels(base)
        results = convolve([f.astype(BF16) for f in fields], first)
        results = [skip[me * count + first + c] * fields[c] + results[c] for c in range(GROUP)]
        if gated:
            results = [g * r for g, r in zip(channels(per_device + base), results)]
        results = [r.reshape(devices, step, LANES) for r in results]
        out[:, base : base + size, :] = jnp.concatenate(results, axis=1).astype(BF16)


def final_kernel(back, gate, out, turned):
    step = gate.shape[0] // LANES
    channels = gate.shape[1]
    turned[...] = back[...].astype(F32).reshape(channels * step, LANES)
    for t in range(step):
        piece = pl.ds(t * LANES, LANES)
        value = turned[pl.ds(t, channels, stride=step), :].T
        out[piece, :] = (gate[piece, :].astype(F32) * value).astype(BF16)


ANY = pl.BlockSpec(memory_space=pl.ANY)
VMEM = pl.BlockSpec(memory_space=pltpu.VMEM)


def run_convolve(skip, values, blocks, gated, tables, n, step, count):
    peers = n // 2
    per_device = count * step
    operands = dict(tables, data=values)
    operands = [operands[name] for name in PARTS + LATER]
    buffers = [
        pltpu.VMEM(o.shape[1:] if name in HALVED else o.shape, o.dtype)
        for name, o in zip(PARTS + LATER, operands)
    ]
    return pl.pallas_call(
        functools.partial(conv_kernel, peers, gated),
        in_specs=[pl.BlockSpec(memory_space=pltpu.SMEM)] + [ANY] * (len(operands) + peers),
        out_specs=VMEM,
        out_shape=jax.ShapeDtypeStruct((n, per_device, LANES), BF16),
        scratch_shapes=buffers
        + [
            pltpu.VMEM((peers,) + blocks[0].shape, BF16),
            pltpu.SemaphoreType.DMA((len(operands) + peers,)),
        ],
        compiler_params=PARAMS,
        cost_estimate=pl.CostEstimate(
            flops=1200 * 1000 * 1000, bytes_accessed=6 * 1024 * 1024, transcendentals=0
        ),
        name="convolve",
    )(skip, *operands, *blocks)


def on_device(signal, gate_one, mix_two, gate_two, skip_one, skip_two, spectrum_one, spectrum_two):
    n = lax.axis_size("ctx")
    peers = n // 2
    length, channels = signal.shape
    step = length // LANES
    count = channels // n
    per_device = count * step
    half_channels = channels // 2

    special_shape = (2, 2, step // 2, LANES, half_channels)
    special = pl.pallas_call(
        special_kernel,
        in_specs=[ANY] * 2,
        out_specs=VMEM,
        out_shape=jax.ShapeDtypeStruct(special_shape, BF16),
        scratch_shapes=[
            pltpu.VMEM((2, 2, length, half_channels), BF16),
            pltpu.VMEM((2, length, half_channels), F32),
            pltpu.SemaphoreType.DMA((2, 2)),
        ],
        compiler_params=PARAMS,
        name="special",
    )(spectrum_one, spectrum_two)
    special = lax.ppermute(special, "ctx", [(0, peers), (peers, 0)])

    data = pl.pallas_call(
        prep_kernel,
        out_shape=jax.ShapeDtypeStruct((n, 2 * per_device, LANES), BF16),
        scratch_shapes=[pltpu.VMEM((channels * step, LANES), F32)],
        compiler_params=PARAMS,
        name="prep",
    )(signal, gate_one, mix_two)
    data, special = lax.optimization_barrier((data, special))
    data = lax.all_to_all(data, "ctx", split_axis=0, concat_axis=0, tiled=True)

    block_shape = (count * 4 * step, LANES)

    def spread(index, spectrum):
        blocks = pl.pallas_call(
            functools.partial(pack_kernel, index),
            in_specs=[ANY, VMEM],
            out_specs=[VMEM] * peers,
            out_shape=[jax.ShapeDtypeStruct(block_shape, BF16)] * peers,
            scratch_shapes=[
                pltpu.VMEM((2, 2, length, half_channels), BF16),
                pltpu.VMEM((2, length, half_channels), F32),
                pltpu.VMEM((half_channels * 4 * step, LANES), F32),
                pltpu.SemaphoreType.DMA((2, 2)),
            ],
            compiler_params=PARAMS,
            name="pack",
        )(spectrum, special)
        return [
            block if s == 0 else lax.ppermute(block, "ctx", [(i, i ^ s) for i in range(n)])
            for s, block in enumerate(blocks)
        ]

    blocks_one = spread(0, spectrum_one)
    blocks_two = spread(1, spectrum_two)
    tables = {name: jnp.asarray(table) for name, table in make_tables(n, step).items()}
    sizes = (tables, n, step, count)
    middle = run_convolve(skip_one, data, blocks_one, True, *sizes)
    out = run_convolve(skip_two, middle, blocks_two, False, *sizes)
    back = lax.all_to_all(out, "ctx", split_axis=0, concat_axis=0, tiled=True)
    return pl.pallas_call(
        final_kernel,
        out_shape=jax.ShapeDtypeStruct((length, channels), BF16),
        scratch_shapes=[pltpu.VMEM((channels * step, LANES), F32)],
        compiler_params=SMALL,
        name="final",
    )(back, gate_two)


def solution(mesh):
    return jax.shard_map(
        on_device,
        mesh=mesh,
        in_specs=(
            P(("group", "ctx"), None),
            P(("group", "ctx"), None),
            P(("group", "ctx"), None),
            P(("group", "ctx"), None),
            P(),
            P(),
            P(None, "ctx", None, None),
            P(None, "ctx", None, None),
        ),
        out_specs=P(("group", "ctx"), None),
        check_vma=False,
    )
```

```python
import functools

import jax
import jax.numpy as jnp
import numpy as np
from jax import lax
from jax.experimental import pallas as pl
from jax.experimental.pallas import tpu as pltpu
from jax.sharding import PartitionSpec as P

F32 = jnp.float32
BF16 = jnp.bfloat16
LANES = 128
GROUP = 8
SMALL = pltpu.CompilerParams(vmem_limit_bytes=24 * 1024 * 1024)
PARAMS = pltpu.CompilerParams(vmem_limit_bytes=60 * 1024 * 1024)


def split_table(table):
    high = table.astype(jnp.bfloat16)
    low = (table - high.astype(np.float64)).astype(jnp.bfloat16)
    return high, low


def make_tables(n, step):
    rows = n * step
    first_len = 2 * rows
    total = first_len * LANES
    turn = 2.0 * np.pi
    n1 = np.arange(rows)
    n2 = np.arange(LANES)
    forward_one, inverse_one, cosines, sines = [], [], [], []
    for half in range(2):
        k1 = np.array(
            [
                2 * (half * (n // 2) + source) + a + 2 * n * low
                for source in range(n // 2)
                for a in range(2)
                for low in range(step)
            ]
        )
        k1[:step] = [2 * n * j for j in range(step // 2)] + [n + 2 * n * j for j in range(step // 2)]
        angle = turn * ((k1[:, None] * n1[None, :]) % first_len) / first_len
        real_rows, imag_rows = np.cos(angle), -np.sin(angle)
        imag_rows[0] = np.cos(np.pi * n1)
        table = np.concatenate([real_rows, imag_rows], axis=0)
        forward_one.append(table)
        weight = np.full((2 * rows, 1), 2.0 / total)
        weight[0] = weight[rows] = 1.0 / total
        inverse_one.append((table * weight).T)
        angle = turn * ((k1[:, None] * n2[None, :]) % total) / total
        angle[0] = 0.0
        cosines.append(np.cos(angle))
        sines.append(-np.sin(angle))
    angle = turn * ((n2[:, None] * n2[None, :]) % LANES) / LANES
    cosine, sine = np.cos(angle), np.sin(angle)
    forward_two = np.block([[cosine, -sine], [sine, cosine]])
    inverse_two = np.block([[cosine, sine], [-sine, cosine]])
    half_lanes = LANES // 2
    even = turn * ((n2[:, None] * np.arange(half_lanes)[None, :]) % LANES) / LANES
    odd = turn * ((n2[:, None] * (1 + 2 * np.arange(half_lanes))[None, :]) % (2 * LANES)) / (2 * LANES)
    zero = np.zeros((LANES, half_lanes))
    even_imag = -np.sin(even)
    even_imag[:, 0] = np.cos(np.pi * n2)
    forward_row = np.block(
        [[np.cos(even), zero, even_imag, zero], [zero, np.cos(odd), zero, -np.sin(odd)]]
    )
    weight = np.full((2 * LANES, 1), 2.0)
    weight[0] = weight[LANES] = 1.0
    inverse_row = (forward_row * weight[:, 0][None, :]).T

    def along_rows(table):
        high, low = split_table(table)
        return np.concatenate([high, low, high], axis=0)

    def along_columns(table):
        high, low = split_table(table)
        return np.concatenate([high, low, high], axis=1)

    def two_columns(table):
        return np.concatenate(split_table(table), axis=1)

    return {
        "forward_one": np.stack([two_columns(t) for t in forward_one]),
        "inverse_one": np.stack([along_columns(t) for t in inverse_one]),
        "turns": np.stack([cosines, sines], axis=1).astype(np.float32),
        "forward_two": along_rows(forward_two),
        "inverse_two": along_rows(inverse_two),
        "forward_row": along_rows(forward_row),
        "inverse_row": along_rows(inverse_row),
    }


def prep_kernel(signal, gate, mix, data, turned):
    step = signal.shape[0] // LANES
    channels = signal.shape[1]
    devices = data.shape[0]
    rows = data.shape[1] // 2
    for part in range(2):
        for t in range(step):
            piece = pl.ds(t * LANES, LANES)
            if part == 0:
                value = signal[piece, :].astype(F32)
            else:
                value = gate[piece, :].astype(F32) * mix[piece, :].astype(F32)
            turned[pl.ds(t, channels, stride=step), :] = value.T
        data[:, part * rows : (part + 1) * rows, :] = (
            turned[...].reshape(devices, rows, LANES).astype(BF16)
        )


def place():
    n = lax.axis_size("ctx")
    me = lax.axis_index("ctx")
    peers = n // 2
    return me, me // peers, lax.rem(me, peers), me == 0, me == peers


def sent_blocks(peers, parity):
    chips = [[s, s + 1] for s in range(2, peers // 2, 2)]
    return [[0], [1]] + chips + [[s + parity] for s in range(peers // 2, peers, 2)]


def held_blocks(peers, parity):
    received = [offsets[0] for offsets in sent_blocks(peers, parity)]
    beside = list(range(3, peers // 2, 2))
    return received + beside + [s + 1 - parity for s in range(peers // 2, peers, 2)]


def special_kernel(spec_one, spec_two, *refs):
    *outs, raw, strided, turned, landed = refs
    parity = lax.rem(lax.axis_index("group"), 2)
    step = spec_one.shape[2] // LANES
    lines = step // 2
    width = raw.shape[3]
    _, half, _, is_first, _ = place()
    columns = pl.ds(pl.multiple_of((1 - half) * width, width), width)
    copies = [
        pltpu.make_async_copy(spec.at[ri, 0, :, columns], raw.at[index, ri], landed.at[index, ri])
        for index, spec in enumerate((spec_one, spec_two))
        for ri in range(2)
    ]
    for copy in copies:
        copy.start()
    for index in range(2):
        for ri in range(2):
            copies[2 * index + ri].wait()
            strided[ri] = raw[index, ri].astype(F32)
        for j in range(lines):
            pair = [strided[ri, pl.ds(j, LANES, stride=step), :] for ri in range(2)]
            if j == 0:
                packed = pack_row(strided, pair[0], pair[1], step)
                pair = [jnp.where(is_first, p, v) for p, v in zip(packed, pair)]
            for ri in range(2):
                turned[index, pl.ds(ri * lines + j, width, stride=step), :] = pair[ri].T
        size = outs[0].shape[2]
        for i, out in enumerate(outs):
            for core in range(2):
                begin = pl.multiple_of((4 * i + 2 * parity + core) * size, size)
                out[core, index] = turned[index, pl.ds(begin, size), :].astype(BF16)


def pack_row(strided, real_part, imag_part, step):
    half = LANES // 2
    odd = [strided[ri, pl.ds(step // 2, LANES, stride=step), :] for ri in range(2)]
    packed_real = jnp.concatenate([real_part[:half], odd[0][:half]], axis=0)
    packed_imag = jnp.concatenate([imag_part[:half], odd[1][:half]], axis=0)
    top = lax.broadcasted_iota(jnp.int32, packed_imag.shape, 0) == 0
    middle = jnp.broadcast_to(real_part[half : half + 1], packed_imag.shape)
    return packed_real, jnp.where(top, middle, packed_imag)


def pack_kernel(spec_one, spec_two, *refs):
    *outs, raw, strided, turned, landed = refs
    peers = lax.axis_size("ctx") // 2
    step = spec_one.shape[2] // LANES
    channels = raw.shape[4]
    _, half, low_index, is_first, is_middle = place()
    parity = lax.rem(lax.axis_index("group"), 2)
    row_count = 2 * step
    columns = pl.ds(pl.multiple_of(half * channels, channels), channels)
    copies = {
        (index, a, ri): pltpu.make_async_copy(
            spec.at[ri, a, :, columns], raw.at[index, a, ri], landed.at[index, a, ri]
        )
        for index, spec in enumerate((spec_one, spec_two))
        for a in range(2)
        for ri in range(2)
    }
    for copy in copies.values():
        copy.start()
    for index in range(2):
        for a in range(2):
            for ri in range(2):
                copies[index, a, ri].wait()
                strided[ri] = raw[index, a, ri].astype(F32)
            for low in range(step):
                pair = [strided[ri, pl.ds(low, LANES, stride=step), :] for ri in range(2)]
                if a == 0 and low == 0:
                    packed = pack_row(strided, pair[0], pair[1], step)
                    pair = [jnp.where(is_first, p, v) for p, v in zip(packed, pair)]
                for ri in range(2):
                    value = pair[ri]
                    if a == 0 and low >= step // 2:
                        own = strided[ri, pl.ds(low - step // 2, LANES, stride=step), :]
                        value = jnp.where(is_middle, own, value)
                    row = ri * row_count + a * step + low
                    turned[pl.ds(row, channels, stride=2 * row_count), :] = value.T
        block = channels // peers * 2 * row_count
        for offsets, out in zip(sent_blocks(peers, parity), outs):
            for i, s in enumerate(offsets):
                start = pl.multiple_of((low_index ^ s) * block, block)
                out[i, index] = turned[pl.ds(start, block), :].astype(BF16)


def split_value(value):
    high = value.astype(BF16)
    return high, (value - high.astype(F32)).astype(BF16)


def split_columns(value):
    high, low = split_value(value)
    return jnp.concatenate([high, high, low], axis=1)


def split_rows(value):
    high, low = split_value(value)
    return jnp.concatenate([high, high, low], axis=0)


def dot(left, right):
    return jnp.dot(left, right, preferred_element_type=F32)


def insert_rows(filters, lacking, half, step):
    lines = step // 2
    shape = (filters.shape[2] // (4 * step), 4 * step, LANES)
    for index in range(2):
        own = lacking[index].astype(F32)
        size = own.shape[0]
        before, after = pltpu.roll(own, lines, 0), pltpu.roll(own, size - lines, 0)
        row = lax.rem(lax.broadcasted_iota(jnp.int32, own.shape, 0), step)
        low = row < lines
        chosen = (low == (half == 1)).reshape(-1, step, LANES)
        real_part = jnp.where(low, own, before).reshape(-1, step, LANES)
        imag_part = jnp.where(low, after, own).reshape(-1, step, LANES)
        old = filters[0, index].astype(F32).reshape(shape)
        new = jnp.concatenate(
            [
                jnp.where(chosen, real_part, old[:, :step]),
                old[:, step : 2 * step],
                jnp.where(chosen, imag_part, old[:, 2 * step : 3 * step]),
                old[:, 3 * step :],
            ],
            axis=1,
        )
        filters[0, index] = new.reshape(filters.shape[2:]).astype(BF16)


HALVED = ("forward_one", "turns", "inverse_one")
PARTS = ("data", "forward_one", "turns", "forward_two", "forward_row")
LATER = ("inverse_two", "inverse_row", "inverse_one")


def conv_kernel(peers, skip_one, skip_two, *refs):
    names = PARTS + LATER
    sources = dict(zip(names, refs))
    blocks, refs = refs[len(names) : len(names) + peers], refs[len(names) + peers :]
    specials, result, refs = refs[:2], refs[2], refs[3:]
    buffers = dict(zip(names, refs))
    filters, lacking, out, landed, left = refs[len(names) :]
    me, half, low_index, _, _ = place()
    copies = {}
    for i, name in enumerate(names):
        source = sources[name].at[half] if name in HALVED else sources[name]
        copies[name] = pltpu.make_async_copy(source, buffers[name], landed.at[i])
    parity = lax.rem(lax.axis_index("group"), 2)
    for i, s in enumerate(held_blocks(peers, parity)):
        copies[i] = pltpu.make_async_copy(
            blocks[i].at[0], filters.at[low_index ^ s], landed.at[len(names) + i]
        )
    for name in PARTS:
        copies[name].start()
    for core, special in enumerate(specials):
        copies["special"] = pltpu.make_async_copy(special, lacking, landed.at[len(names) + peers])

        @pl.when(lax.rem(me, 2) == core)
        def _():
            copies["special"].start()

    for name in tuple(range(peers)) + LATER:
        copies[name].start()
    awaited = set()

    def need(*wanted):
        for name in wanted:
            if name not in awaited:
                awaited.add(name)
                copies[name].wait()

    data, turns = buffers["data"], buffers["turns"]
    devices = data.shape[0]
    per_device = out.shape[1]
    rows = turns.shape[1]
    step = rows // devices
    count = per_device // step
    row_count = 2 * step
    top_row = lax.broadcasted_iota(jnp.int32, (step, 2 * LANES), 0) == 0
    corner = top_row[:, :LANES] & (lax.broadcasted_iota(jnp.int32, (step, LANES), 1) == 0)

    def with_top(values, tops):
        return [
            jnp.concatenate(
                [jnp.where(top_row, tops[c * step : (c + 1) * step], v[:step]), v[step:]], axis=0
            )
            for c, v in enumerate(values)
        ]

    def second_stage(values, table, row_table):
        need(table, row_table)
        main = dot(split_columns(jnp.concatenate(values, axis=0)), buffers[table][...])
        tops = dot(split_columns(jnp.concatenate([v[:step] for v in values], axis=0)), buffers[row_table][...])
        return with_top([main[c * rows : (c + 1) * rows] for c in range(GROUP)], tops)

    def convolve(fields, layer, first):
        joined = jnp.concatenate(fields, axis=1)
        need("forward_one", "turns")
        cosine, sine = turns[0], turns[1]
        staged = dot(buffers["forward_one"][...], jnp.concatenate([joined, joined], axis=0))
        turned = []
        for c in range(GROUP):
            lanes = slice(c * LANES, (c + 1) * LANES)
            real_part, imag_part = staged[:rows, lanes], staged[rows:, lanes]
            turned.append(
                jnp.concatenate(
                    [
                        real_part * cosine - imag_part * sine,
                        real_part * sine + imag_part * cosine,
                    ],
                    axis=1,
                )
            )
        spectral = second_stage(turned, "forward_two", "forward_row")
        if "special" not in awaited:
            need("special", *range(peers))
            insert_rows(filters, lacking, half, step)
        products = []
        for c in range(GROUP):
            start = (first + c) * 2 * row_count
            stored = filters[:, layer, start : start + 2 * row_count, :]
            h_real = stored[:, :row_count].reshape(rows, LANES).astype(F32)
            h_imag = stored[:, row_count:].reshape(rows, LANES).astype(F32)
            x_real, x_imag = spectral[c][:, :LANES], spectral[c][:, LANES:]
            real_real, imag_imag = x_real * h_real, x_imag * h_imag
            y_real = real_real - imag_imag
            y_imag = x_real * h_imag + x_imag * h_real
            y_real = jnp.concatenate(
                [jnp.where(corner, real_real[:step], y_real[:step]), y_real[step:]], axis=0
            )
            y_imag = jnp.concatenate(
                [jnp.where(corner, imag_imag[:step], y_imag[:step]), y_imag[step:]], axis=0
            )
            products.append(jnp.concatenate([y_real, y_imag], axis=1))
        inverted = second_stage(products, "inverse_two", "inverse_row")
        columns = []
        for c in range(GROUP):
            real_part, imag_part = inverted[c][:, :LANES], inverted[c][:, LANES:]
            columns.append(
                jnp.concatenate(
                    [
                        real_part * cosine + imag_part * sine,
                        imag_part * cosine - real_part * sine,
                    ],
                    axis=0,
                )
            )
        need("inverse_one")
        result = dot(buffers["inverse_one"][...], split_rows(jnp.concatenate(columns, axis=1)))
        return [result[:, c * LANES : (c + 1) * LANES] for c in range(GROUP)]

    need("data")
    size = GROUP * step
    writes = []
    for first in range(0, count, GROUP):

        def channels(start):
            values = data[:, start : start + size, :].astype(F32)
            return [
                values[:, c * step : (c + 1) * step, :].reshape(rows, LANES) for c in range(GROUP)
            ]

        base = first * step
        place_of = me * count + first
        fields = channels(base)
        results = convolve([f.astype(BF16) for f in fields], 0, first)
        middles = [
            (g * (r + skip_one[place_of + c] * f)).astype(BF16)
            for c, (g, r, f) in enumerate(zip(channels(per_device + base), results, fields))
        ]
        results = convolve(middles, 1, first)
        results = [
            (r + skip_two[place_of + c] * m.astype(F32)).reshape(devices, step, LANES)
            for c, (r, m) in enumerate(zip(results, middles))
        ]
        out[:, base : base + size, :] = jnp.concatenate(results, axis=1).astype(BF16)
        part = (slice(None), pl.ds(base, size))
        writes.append(pltpu.make_async_copy(out.at[part], result.at[part], left.at[len(writes)]))
        writes[-1].start()
    for write in writes:
        write.wait()


def final_kernel(back, gate, out, turned):
    step = gate.shape[0] // LANES
    channels = gate.shape[1]
    turned[...] = back[...].astype(F32).reshape(channels * step, LANES)
    for t in range(step):
        piece = pl.ds(t * LANES, LANES)
        value = turned[pl.ds(t, channels, stride=step), :].T
        out[piece, :] = (gate[piece, :].astype(F32) * value).astype(BF16)


ANY = pl.BlockSpec(memory_space=pl.ANY)
VMEM = pl.BlockSpec(memory_space=pltpu.VMEM)


def run_convolve(skips, data, blocks, specials, tables, n, step, count):
    peers = n // 2
    per_device = count * step
    operands = dict(tables, data=data)
    operands = [operands[name] for name in PARTS + LATER]
    buffers = [
        pltpu.VMEM(o.shape[1:] if name in HALVED else o.shape, o.dtype)
        for name, o in zip(PARTS + LATER, operands)
    ]
    return pl.pallas_call(
        functools.partial(conv_kernel, peers),
        in_specs=[pl.BlockSpec(memory_space=pltpu.SMEM)] * 2 + [ANY] * (len(operands) + peers + 2),
        out_specs=ANY,
        out_shape=jax.ShapeDtypeStruct((n, per_device, LANES), BF16),
        scratch_shapes=buffers
        + [
            pltpu.VMEM((peers,) + blocks[0].shape[1:], BF16),
            pltpu.VMEM(specials[0].shape, BF16),
            pltpu.VMEM((n, per_device, LANES), BF16),
            pltpu.SemaphoreType.DMA((len(operands) + peers + 1,)),
            pltpu.SemaphoreType.DMA((count // GROUP,)),
        ],
        compiler_params=PARAMS,
        cost_estimate=pl.CostEstimate(
            flops=2400 * 1000 * 1000, bytes_accessed=8 * 1024 * 1024, transcendentals=0
        ),
        name="convolve",
    )(*skips, *operands, *blocks, *specials)


def on_device(signal, gate_one, mix_two, gate_two, skip_one, skip_two, spectrum_one, spectrum_two):
    n = lax.axis_size("ctx")
    groups = lax.axis_size("group")
    peers = n // 2
    length, channels = signal.shape
    step = length // LANES
    count = channels // n
    per_device = count * step
    half_channels = channels // 2

    data = pl.pallas_call(
        prep_kernel,
        out_shape=jax.ShapeDtypeStruct((n, 2 * per_device, LANES), BF16),
        scratch_shapes=[pltpu.VMEM((channels * step, LANES), F32)],
        compiler_params=PARAMS,
        name="prep",
    )(signal, gate_one, mix_two)

    both = ("group", "ctx")
    block_shape = (2, count * 4 * step, LANES)
    shapes = [(len(offsets),) + block_shape for offsets in sent_blocks(peers, 0)]
    blocks = pl.pallas_call(
        pack_kernel,
        in_specs=[ANY, ANY],
        out_specs=[VMEM] * len(shapes),
        out_shape=[jax.ShapeDtypeStruct(shape, BF16) for shape in shapes],
        scratch_shapes=[
            pltpu.VMEM((2, 2, 2, length, half_channels), BF16),
            pltpu.VMEM((2, length, half_channels), F32),
            pltpu.VMEM((half_channels * 4 * step, LANES), F32),
            pltpu.SemaphoreType.DMA((2, 2, 2)),
        ],
        compiler_params=PARAMS,
        name="pack",
    )(spectrum_one, spectrum_two)
    routes = [[offsets[0] for offsets in sent_blocks(peers, g % 2)] for g in range(groups)]
    received = [
        lax.ppermute(
            block, both, [(g * n + d, g * n + (d ^ routes[g][i])) for g in range(groups) for d in range(n)]
        )
        if i
        else block
        for i, block in enumerate(blocks)
    ]
    mates = [(d, d ^ 1) for d in range(n)]
    swap = [(g, g ^ 1) for g in range(groups)]
    far = 1 + peers // 4
    passed = [lax.ppermute(block, "group", swap) for block in received[far:]]
    beside = [lax.ppermute(block[1:], "ctx", mates) for block in received[2:far]]

    lacked = pl.pallas_call(
        special_kernel,
        in_specs=[ANY] * 2,
        out_specs=[VMEM] * (peers // 4),
        out_shape=[jax.ShapeDtypeStruct((2, 2, per_device, LANES), BF16)] * (peers // 4),
        scratch_shapes=[
            pltpu.VMEM((2, 2, length, half_channels), BF16),
            pltpu.VMEM((2, length, half_channels), F32),
            pltpu.VMEM((2, half_channels * step, LANES), F32),
            pltpu.SemaphoreType.DMA((2, 2)),
        ],
        compiler_params=PARAMS,
        name="special",
    )(spectrum_one, spectrum_two)
    lacked = [
        lax.ppermute(
            rows,
            both,
            [
                (g * n + peers - end, g * n + end + 4 * i + 2 * (g % 2))
                for g in range(groups)
                for end in (0, peers)
            ],
        )
        for i, rows in enumerate(lacked)
    ]
    lacked = sum(lacked[1:], lacked[0])
    others = lax.ppermute(lacked, "group", swap)
    others, passed[0] = lax.optimization_barrier((others, passed[0]))
    lacked = lacked + others
    mine = (lacked[0], lax.ppermute(lacked[1], "ctx", [(d, d + 1) for d in range(0, n, 2)]))
    data = lax.all_to_all(data, "ctx", split_axis=0, concat_axis=0, tiled=True)
    held = received + beside + passed
    tables = {name: jnp.asarray(table) for name, table in make_tables(n, step).items()}
    skips = (skip_one, skip_two)
    out = run_convolve(skips, data, held, mine, tables, n, step, count)
    back = lax.all_to_all(out, "ctx", split_axis=0, concat_axis=0, tiled=True)
    return pl.pallas_call(
        final_kernel,
        out_shape=jax.ShapeDtypeStruct((length, channels), BF16),
        scratch_shapes=[pltpu.VMEM((channels * step, LANES), F32)],
        compiler_params=SMALL,
        name="final",
    )(back, gate_two)


def solution(mesh):
    return jax.shard_map(
        on_device,
        mesh=mesh,
        in_specs=(
            P(("group", "ctx"), None),
            P(("group", "ctx"), None),
            P(("group", "ctx"), None),
            P(("group", "ctx"), None),
            P(),
            P(),
            P(None, "ctx", None, None),
            P(None, "ctx", None, None),
        ),
        out_specs=P(("group", "ctx"), None),
        check_vma=False,
    )
```

```python
import functools

import jax
import jax.numpy as jnp
import numpy as np
from jax import lax
from jax.experimental import pallas as pl
from jax.experimental.pallas import tpu as pltpu
from jax.sharding import PartitionSpec as P

F32 = jnp.float32
BF16 = jnp.bfloat16
LANES = 128
GROUP = 8
SMALL = pltpu.CompilerParams(vmem_limit_bytes=24 * 1024 * 1024)
PARAMS = pltpu.CompilerParams(vmem_limit_bytes=60 * 1024 * 1024)


def split_table(table):
    high = table.astype(jnp.bfloat16)
    low = (table - high.astype(np.float64)).astype(jnp.bfloat16)
    return high, low


def make_tables(n, step):
    rows = n * step
    first_len = 2 * rows
    total = first_len * LANES
    turn = 2.0 * np.pi
    n1 = np.arange(rows)
    n2 = np.arange(LANES)
    forward_one, inverse_one, cosines, sines = [], [], [], []
    for half in range(2):
        k1 = np.array(
            [
                2 * (half * (n // 2) + source) + a + 2 * n * low
                for source in range(n // 2)
                for a in range(2)
                for low in range(step)
            ]
        )
        k1[:step] = [2 * n * j for j in range(step // 2)] + [n + 2 * n * j for j in range(step // 2)]
        angle = turn * ((k1[:, None] * n1[None, :]) % first_len) / first_len
        real_rows, imag_rows = np.cos(angle), -np.sin(angle)
        imag_rows[0] = np.cos(np.pi * n1)
        table = np.concatenate([real_rows, imag_rows], axis=0)
        forward_one.append(table)
        weight = np.full((2 * rows, 1), 2.0 / total)
        weight[0] = weight[rows] = 1.0 / total
        inverse_one.append((table * weight).T)
        angle = turn * ((k1[:, None] * n2[None, :]) % total) / total
        angle[0] = 0.0
        cosines.append(np.cos(angle))
        sines.append(-np.sin(angle))
    angle = turn * ((n2[:, None] * n2[None, :]) % LANES) / LANES
    cosine, sine = np.cos(angle), np.sin(angle)
    forward_two = np.block([[cosine, -sine], [sine, cosine]])
    inverse_two = np.block([[cosine, sine], [-sine, cosine]])
    half_lanes = LANES // 2
    even = turn * ((n2[:, None] * np.arange(half_lanes)[None, :]) % LANES) / LANES
    odd = turn * ((n2[:, None] * (1 + 2 * np.arange(half_lanes))[None, :]) % (2 * LANES)) / (2 * LANES)
    zero = np.zeros((LANES, half_lanes))
    even_imag = -np.sin(even)
    even_imag[:, 0] = np.cos(np.pi * n2)
    forward_row = np.block(
        [[np.cos(even), zero, even_imag, zero], [zero, np.cos(odd), zero, -np.sin(odd)]]
    )
    weight = np.full((2 * LANES, 1), 2.0)
    weight[0] = weight[LANES] = 1.0
    inverse_row = (forward_row * weight[:, 0][None, :]).T

    def along_rows(table):
        high, low = split_table(table)
        return np.concatenate([high, low, high], axis=0)

    def along_columns(table):
        high, low = split_table(table)
        return np.concatenate([high, low, high], axis=1)

    def two_columns(table):
        return np.concatenate(split_table(table), axis=1)

    return {
        "forward_one": np.stack([two_columns(t) for t in forward_one]),
        "inverse_one": np.stack([along_columns(t) for t in inverse_one]),
        "turns": np.stack([cosines, sines], axis=1).astype(np.float32),
        "forward_two": along_rows(forward_two),
        "inverse_two": along_rows(inverse_two),
        "forward_row": along_rows(forward_row),
        "inverse_row": along_rows(inverse_row),
    }


def prep_kernel(signal, gate, mix, result, raw, turned, data, landed, left):
    step = raw.shape[1] // LANES
    channels = raw.shape[2]
    rows = data.shape[1] // 2
    copies = [
        pltpu.make_async_copy(source, raw.at[i], landed.at[i])
        for i, source in enumerate((signal, gate, mix))
    ]
    for copy in copies:
        copy.start()
    writes = []
    for part in range(2):
        for copy in copies[1:] if part else copies[:1]:
            copy.wait()
        for t in range(step):
            piece = pl.ds(t * LANES, LANES)
            if part == 0:
                value = raw[0, piece, :].astype(F32)
            else:
                value = raw[1, piece, :].astype(F32) * raw[2, piece, :].astype(F32)
            turned[pl.ds(t, channels, stride=step), :] = value.T
        half = (slice(None), pl.ds(part * rows, rows))
        data[half] = turned[: channels * step].reshape(data.shape[0], rows, LANES).astype(BF16)
        writes.append(pltpu.make_async_copy(data.at[half], result.at[half], left.at[part]))
        writes[part].start()
    for write in writes:
        write.wait()


def place():
    n = lax.axis_size("ctx")
    me = lax.axis_index("ctx")
    peers = n // 2
    return me, me // peers, lax.rem(me, peers), me == 0, me == peers


def sent_blocks(peers, parity):
    chips = [[s, s + 1] for s in range(2, peers // 2, 2)]
    return [[0], [1]] + chips + [[s + parity] for s in range(peers // 2, peers, 2)]


def held_blocks(peers, parity):
    received = [offsets[0] for offsets in sent_blocks(peers, parity)]
    beside = list(range(3, peers // 2, 2))
    return received + beside + [s + 1 - parity for s in range(peers // 2, peers, 2)]


def special_kernel(spec_one, spec_two, *refs):
    *outs, raw, strided, turned, landed = refs
    parity = lax.rem(lax.axis_index("group"), 2)
    step = spec_one.shape[2] // LANES
    lines = step // 2
    width = raw.shape[3]
    _, half, _, is_first, _ = place()
    columns = pl.ds(pl.multiple_of((1 - half) * width, width), width)
    copies = [
        pltpu.make_async_copy(spec.at[ri, 0, :, columns], raw.at[index, ri], landed.at[index, ri])
        for index, spec in enumerate((spec_one, spec_two))
        for ri in range(2)
    ]
    for copy in copies:
        copy.start()
    for index in range(2):
        for ri in range(2):
            copies[2 * index + ri].wait()
            strided[ri, : raw.shape[2]] = raw[index, ri].astype(F32)
        for j in range(lines):
            pair = [strided[ri, pl.ds(j, LANES, stride=step), :] for ri in range(2)]
            if j == 0:
                packed = pack_row(strided, pair[0], pair[1], step)
                pair = [jnp.where(is_first, p, v) for p, v in zip(packed, pair)]
            for ri in range(2):
                turned[index, pl.ds(ri * lines + j, width, stride=step), :] = pair[ri].T
        size = outs[0].shape[2]
        for i, out in enumerate(outs):
            for core in range(2):
                begin = pl.multiple_of((4 * i + 2 * parity + core) * size, size)
                out[core, index] = turned[index, pl.ds(begin, size), :].astype(BF16)


def pack_row(strided, real_part, imag_part, step):
    half = LANES // 2
    odd = [strided[ri, pl.ds(step // 2, LANES, stride=step), :] for ri in range(2)]
    packed_real = jnp.concatenate([real_part[:half], odd[0][:half]], axis=0)
    packed_imag = jnp.concatenate([imag_part[:half], odd[1][:half]], axis=0)
    top = lax.broadcasted_iota(jnp.int32, packed_imag.shape, 0) == 0
    middle = jnp.broadcast_to(real_part[half : half + 1], packed_imag.shape)
    return packed_real, jnp.where(top, middle, packed_imag)


def pack_kernel(spec_one, spec_two, *refs):
    *outs, raw, strided, turned, landed = refs
    peers = lax.axis_size("ctx") // 2
    step = spec_one.shape[2] // LANES
    channels = raw.shape[4]
    _, half, low_index, is_first, is_middle = place()
    parity = lax.rem(lax.axis_index("group"), 2)
    row_count = 2 * step
    columns = pl.ds(pl.multiple_of(half * channels, channels), channels)
    copies = {
        (index, a, ri): pltpu.make_async_copy(
            spec.at[ri, a, :, columns], raw.at[index, a, ri], landed.at[index, a, ri]
        )
        for index, spec in enumerate((spec_one, spec_two))
        for a in range(2)
        for ri in range(2)
    }
    for copy in copies.values():
        copy.start()
    for index in range(2):
        for a in range(2):
            for ri in range(2):
                copies[index, a, ri].wait()
                strided[ri, : raw.shape[3]] = raw[index, a, ri].astype(F32)
            for low in range(step):
                pair = [strided[ri, pl.ds(low, LANES, stride=step), :] for ri in range(2)]
                if a == 0 and low == 0:
                    packed = pack_row(strided, pair[0], pair[1], step)
                    pair = [jnp.where(is_first, p, v) for p, v in zip(packed, pair)]
                for ri in range(2):
                    value = pair[ri]
                    if a == 0 and low >= step // 2:
                        own = strided[ri, pl.ds(low - step // 2, LANES, stride=step), :]
                        value = jnp.where(is_middle, own, value)
                    row = ri * row_count + a * step + low
                    turned[pl.ds(row, channels, stride=2 * row_count), :] = value.T
        block = channels // peers * 2 * row_count
        for offsets, out in zip(sent_blocks(peers, parity), outs):
            for i, s in enumerate(offsets):
                start = pl.multiple_of((low_index ^ s) * block, block)
                out[i, index] = turned[pl.ds(start, block), :].astype(BF16)


def split_value(value):
    high = value.astype(BF16)
    return high, (value - high.astype(F32)).astype(BF16)


def split_columns(value):
    high, low = split_value(value)
    return jnp.concatenate([high, high, low], axis=1)


def split_rows(value):
    high, low = split_value(value)
    return jnp.concatenate([high, high, low], axis=0)


def dot(left, right):
    return jnp.dot(left, right, preferred_element_type=F32)


def insert_rows(filters, lacking, half, step):
    lines = step // 2
    shape = (filters.shape[2] // (4 * step), 4 * step, LANES)
    for index in range(2):
        own = lacking[index].astype(F32)
        size = own.shape[0]
        before, after = pltpu.roll(own, lines, 0), pltpu.roll(own, size - lines, 0)
        row = lax.rem(lax.broadcasted_iota(jnp.int32, own.shape, 0), step)
        low = row < lines
        chosen = (low == (half == 1)).reshape(-1, step, LANES)
        real_part = jnp.where(low, own, before).reshape(-1, step, LANES)
        imag_part = jnp.where(low, after, own).reshape(-1, step, LANES)
        old = filters[0, index].astype(F32).reshape(shape)
        new = jnp.concatenate(
            [
                jnp.where(chosen, real_part, old[:, :step]),
                old[:, step : 2 * step],
                jnp.where(chosen, imag_part, old[:, 2 * step : 3 * step]),
                old[:, 3 * step :],
            ],
            axis=1,
        )
        filters[0, index] = new.reshape(filters.shape[2:]).astype(BF16)


HALVED = ("forward_one", "turns", "inverse_one")
PARTS = ("data", "forward_one", "turns", "forward_two", "forward_row")
LATER = ("inverse_two", "inverse_row", "inverse_one")


def conv_kernel(peers, skip_one, skip_two, *refs):
    names = PARTS + LATER
    sources = dict(zip(names, refs))
    blocks, refs = refs[len(names) : len(names) + peers], refs[len(names) + peers :]
    specials, result, refs = refs[:2], refs[2], refs[3:]
    buffers = dict(zip(names, refs))
    filters, lacking, out, landed, left = refs[len(names) :]
    me, half, low_index, _, _ = place()
    copies = {}
    for i, name in enumerate(names):
        source = sources[name].at[half] if name in HALVED else sources[name]
        copies[name] = pltpu.make_async_copy(source, buffers[name], landed.at[i])
    parity = lax.rem(lax.axis_index("group"), 2)
    for i, s in enumerate(held_blocks(peers, parity)):
        copies[i] = pltpu.make_async_copy(
            blocks[i].at[0], filters.at[low_index ^ s], landed.at[len(names) + i]
        )
    for name in PARTS:
        copies[name].start()
    for core, special in enumerate(specials):
        copies["special"] = pltpu.make_async_copy(special, lacking, landed.at[len(names) + peers])

        @pl.when(lax.rem(me, 2) == core)
        def _():
            copies["special"].start()

    for name in tuple(range(peers)) + LATER:
        copies[name].start()
    awaited = set()

    def need(*wanted):
        for name in wanted:
            if name not in awaited:
                awaited.add(name)
                copies[name].wait()

    data, turns = buffers["data"], buffers["turns"]
    devices = data.shape[0]
    per_device = out.shape[1]
    rows = turns.shape[1]
    step = rows // devices
    count = per_device // step
    row_count = 2 * step
    top_row = lax.broadcasted_iota(jnp.int32, (step, 2 * LANES), 0) == 0
    corner = top_row[:, :LANES] & (lax.broadcasted_iota(jnp.int32, (step, LANES), 1) == 0)

    def with_top(values, tops):
        return [
            jnp.concatenate(
                [jnp.where(top_row, tops[c * step : (c + 1) * step], v[:step]), v[step:]], axis=0
            )
            for c, v in enumerate(values)
        ]

    def second_stage(values, table, row_table):
        need(table, row_table)
        main = dot(split_columns(jnp.concatenate(values, axis=0)), buffers[table][...])
        tops = dot(split_columns(jnp.concatenate([v[:step] for v in values], axis=0)), buffers[row_table][...])
        return with_top([main[c * rows : (c + 1) * rows] for c in range(GROUP)], tops)

    def convolve(fields, layer, first):
        joined = jnp.concatenate(fields, axis=1)
        need("forward_one", "turns")
        cosine, sine = turns[0], turns[1]
        staged = dot(buffers["forward_one"][...], jnp.concatenate([joined, joined], axis=0))
        turned = []
        for c in range(GROUP):
            lanes = slice(c * LANES, (c + 1) * LANES)
            real_part, imag_part = staged[:rows, lanes], staged[rows:, lanes]
            turned.append(
                jnp.concatenate(
                    [
                        real_part * cosine - imag_part * sine,
                        real_part * sine + imag_part * cosine,
                    ],
                    axis=1,
                )
            )
        spectral = second_stage(turned, "forward_two", "forward_row")
        if "special" not in awaited:
            need("special", *range(peers))
            insert_rows(filters, lacking, half, step)
        products = []
        for c in range(GROUP):
            start = (first + c) * 2 * row_count
            stored = filters[:, layer, start : start + 2 * row_count, :]
            h_real = stored[:, :row_count].reshape(rows, LANES).astype(F32)
            h_imag = stored[:, row_count:].reshape(rows, LANES).astype(F32)
            x_real, x_imag = spectral[c][:, :LANES], spectral[c][:, LANES:]
            real_real, imag_imag = x_real * h_real, x_imag * h_imag
            y_real = real_real - imag_imag
            y_imag = x_real * h_imag + x_imag * h_real
            y_real = jnp.concatenate(
                [jnp.where(corner, real_real[:step], y_real[:step]), y_real[step:]], axis=0
            )
            y_imag = jnp.concatenate(
                [jnp.where(corner, imag_imag[:step], y_imag[:step]), y_imag[step:]], axis=0
            )
            products.append(jnp.concatenate([y_real, y_imag], axis=1))
        inverted = second_stage(products, "inverse_two", "inverse_row")
        columns = []
        for c in range(GROUP):
            real_part, imag_part = inverted[c][:, :LANES], inverted[c][:, LANES:]
            columns.append(
                jnp.concatenate(
                    [
                        real_part * cosine + imag_part * sine,
                        imag_part * cosine - real_part * sine,
                    ],
                    axis=0,
                )
            )
        need("inverse_one")
        result = dot(buffers["inverse_one"][...], split_rows(jnp.concatenate(columns, axis=1)))
        return [result[:, c * LANES : (c + 1) * LANES] for c in range(GROUP)]

    need("data")
    size = GROUP * step
    writes = []
    for first in range(0, count, GROUP):

        def channels(start):
            values = data[:, start : start + size, :].astype(F32)
            return [
                values[:, c * step : (c + 1) * step, :].reshape(rows, LANES) for c in range(GROUP)
            ]

        base = first * step
        place_of = me * count + first
        fields = channels(base)
        results = convolve([f.astype(BF16) for f in fields], 0, first)
        middles = [
            (g * (r + skip_one[place_of + c] * f)).astype(BF16)
            for c, (g, r, f) in enumerate(zip(channels(per_device + base), results, fields))
        ]
        results = convolve(middles, 1, first)
        results = [
            (r + skip_two[place_of + c] * m.astype(F32)).reshape(devices, step, LANES)
            for c, (r, m) in enumerate(zip(results, middles))
        ]
        out[:, base : base + size, :] = jnp.concatenate(results, axis=1).astype(BF16)
        part = (slice(None), pl.ds(base, size))
        writes.append(pltpu.make_async_copy(out.at[part], result.at[part], left.at[len(writes)]))
        writes[-1].start()
    for write in writes:
        write.wait()


def final_kernel(back, gate, out, turned):
    step = gate.shape[0] // LANES
    channels = gate.shape[1]
    turned[: channels * step] = back[...].astype(F32).reshape(channels * step, LANES)
    for t in range(step):
        piece = pl.ds(t * LANES, LANES)
        value = turned[pl.ds(t, channels, stride=step), :].T
        out[piece, :] = (gate[piece, :].astype(F32) * value).astype(BF16)


ANY = pl.BlockSpec(memory_space=pl.ANY)
VMEM = pl.BlockSpec(memory_space=pltpu.VMEM)


def run_convolve(skips, data, blocks, specials, tables, n, step, count):
    peers = n // 2
    per_device = count * step
    operands = dict(tables, data=data)
    operands = [operands[name] for name in PARTS + LATER]
    buffers = [
        pltpu.VMEM(o.shape[1:] if name in HALVED else o.shape, o.dtype)
        for name, o in zip(PARTS + LATER, operands)
    ]
    return pl.pallas_call(
        functools.partial(conv_kernel, peers),
        in_specs=[pl.BlockSpec(memory_space=pltpu.SMEM)] * 2 + [ANY] * (len(operands) + peers + 2),
        out_specs=ANY,
        out_shape=jax.ShapeDtypeStruct((n, per_device, LANES), BF16),
        scratch_shapes=buffers
        + [
            pltpu.VMEM((peers,) + blocks[0].shape[1:], BF16),
            pltpu.VMEM(specials[0].shape, BF16),
            pltpu.VMEM((n, per_device, LANES), BF16),
            pltpu.SemaphoreType.DMA((len(operands) + peers + 1,)),
            pltpu.SemaphoreType.DMA((count // GROUP,)),
        ],
        compiler_params=PARAMS,
        cost_estimate=pl.CostEstimate(
            flops=2400 * 1000 * 1000, bytes_accessed=8 * 1024 * 1024, transcendentals=0
        ),
        name="convolve",
    )(*skips, *operands, *blocks, *specials)


def on_device(signal, gate_one, mix_two, gate_two, skip_one, skip_two, spectrum_one, spectrum_two):
    n = lax.axis_size("ctx")
    groups = lax.axis_size("group")
    peers = n // 2
    length, channels = signal.shape
    step = length // LANES
    count = channels // n
    per_device = count * step
    half_channels = channels // 2

    data_shape = (n, 2 * per_device, LANES)
    data = pl.pallas_call(
        prep_kernel,
        in_specs=[ANY] * 3,
        out_specs=ANY,
        out_shape=jax.ShapeDtypeStruct(data_shape, BF16),
        scratch_shapes=[
            pltpu.VMEM((3, length, channels), BF16),
            pltpu.VMEM(((channels + 1) * step, LANES), F32),
            pltpu.VMEM(data_shape, BF16),
            pltpu.SemaphoreType.DMA((3,)),
            pltpu.SemaphoreType.DMA((2,)),
        ],
        compiler_params=PARAMS,
        name="prep",
    )(signal, gate_one, mix_two)

    both = ("group", "ctx")
    block_shape = (2, count * 4 * step, LANES)
    shapes = [(len(offsets),) + block_shape for offsets in sent_blocks(peers, 0)]
    blocks = pl.pallas_call(
        pack_kernel,
        in_specs=[ANY, ANY],
        out_specs=[VMEM] * len(shapes),
        out_shape=[jax.ShapeDtypeStruct(shape, BF16) for shape in shapes],
        scratch_shapes=[
            pltpu.VMEM((2, 2, 2, length, half_channels), BF16),
            pltpu.VMEM((2, length + step, half_channels), F32),
            pltpu.VMEM(((half_channels + 1) * 4 * step, LANES), F32),
            pltpu.SemaphoreType.DMA((2, 2, 2)),
        ],
        compiler_params=PARAMS,
        name="pack",
    )(spectrum_one, spectrum_two)
    routes = [[offsets[0] for offsets in sent_blocks(peers, g % 2)] for g in range(groups)]
    received = [
        lax.ppermute(
            block, both, [(g * n + d, g * n + (d ^ routes[g][i])) for g in range(groups) for d in range(n)]
        )
        if i
        else block
        for i, block in enumerate(blocks)
    ]
    mates = [(d, d ^ 1) for d in range(n)]
    swap = [(g, g ^ 1) for g in range(groups)]
    far = 1 + peers // 4
    passed = [lax.ppermute(block, "group", swap) for block in received[far:]]
    beside = [lax.ppermute(block[1:], "ctx", mates) for block in received[2:far]]

    lacked = pl.pallas_call(
        special_kernel,
        in_specs=[ANY] * 2,
        out_specs=[VMEM] * (peers // 4),
        out_shape=[jax.ShapeDtypeStruct((2, 2, per_device, LANES), BF16)] * (peers // 4),
        scratch_shapes=[
            pltpu.VMEM((2, 2, length, half_channels), BF16),
            pltpu.VMEM((2, length + step, half_channels), F32),
            pltpu.VMEM((2, (half_channels + 1) * step, LANES), F32),
            pltpu.SemaphoreType.DMA((2, 2)),
        ],
        compiler_params=PARAMS,
        name="special",
    )(spectrum_one, spectrum_two)
    lacked = [
        lax.ppermute(
            rows,
            both,
            [
                (g * n + peers - end, g * n + end + 4 * i + 2 * (g % 2))
                for g in range(groups)
                for end in (0, peers)
            ],
        )
        for i, rows in enumerate(lacked)
    ]
    lacked = sum(lacked[1:], lacked[0])
    holders = [(g, d) for g in range(groups) for d in range(0, n, 2) if d // 2 % 2 == g % 2]
    others = lax.ppermute(lacked, both, [(g * n + d, (g ^ 1) * n + d) for g, d in holders])
    others, passed[0] = lax.optimization_barrier((others, passed[0]))
    lacked = lacked + others
    mine = (lacked[0], lax.ppermute(lacked[1], "ctx", [(d, d + 1) for d in range(0, n, 2)]))
    data = lax.all_to_all(data, "ctx", split_axis=0, concat_axis=0, tiled=True)
    held = received + beside + passed
    tables = {name: jnp.asarray(table) for name, table in make_tables(n, step).items()}
    skips = (skip_one, skip_two)
    out = run_convolve(skips, data, held, mine, tables, n, step, count)
    back = lax.all_to_all(out, "ctx", split_axis=0, concat_axis=0, tiled=True)
    return pl.pallas_call(
        final_kernel,
        out_shape=jax.ShapeDtypeStruct((length, channels), BF16),
        scratch_shapes=[pltpu.VMEM(((channels + 1) * step, LANES), F32)],
        compiler_params=SMALL,
        name="final",
    )(back, gate_two)


def solution(mesh):
    return jax.shard_map(
        on_device,
        mesh=mesh,
        in_specs=(
            P(("group", "ctx"), None),
            P(("group", "ctx"), None),
            P(("group", "ctx"), None),
            P(("group", "ctx"), None),
            P(),
            P(),
            P(None, "ctx", None, None),
            P(None, "ctx", None, None),
        ),
        out_specs=P(("group", "ctx"), None),
        check_vma=False,
    )
```

```python
import functools

import jax
import jax.numpy as jnp
import numpy as np
from jax import lax
from jax.experimental import pallas as pl
from jax.experimental.pallas import tpu as pltpu
from jax.sharding import PartitionSpec as P

F32 = jnp.float32
BF16 = jnp.bfloat16
LANES = 128
GROUP = 8
SMALL = pltpu.CompilerParams(vmem_limit_bytes=24 * 1024 * 1024)
PARAMS = pltpu.CompilerParams(vmem_limit_bytes=60 * 1024 * 1024)


def split_table(table):
    high = table.astype(jnp.bfloat16)
    low = (table - high.astype(np.float64)).astype(jnp.bfloat16)
    return high, low


def make_tables(n, step):
    rows = n * step
    first_len = 2 * rows
    total = first_len * LANES
    turn = 2.0 * np.pi
    n1 = np.arange(rows)
    n2 = np.arange(LANES)
    forward_one, inverse_one, cosines, sines = [], [], [], []
    for half in range(2):
        k1 = np.array(
            [
                2 * (half * (n // 2) + source) + a + 2 * n * low
                for source in range(n // 2)
                for a in range(2)
                for low in range(step)
            ]
        )
        k1[:step] = [2 * n * j for j in range(step // 2)] + [n + 2 * n * j for j in range(step // 2)]
        angle = turn * ((k1[:, None] * n1[None, :]) % first_len) / first_len
        real_rows, imag_rows = np.cos(angle), -np.sin(angle)
        imag_rows[0] = np.cos(np.pi * n1)
        table = np.concatenate([real_rows, imag_rows], axis=0)
        forward_one.append(table)
        weight = np.full((2 * rows, 1), 2.0 / total)
        weight[0] = weight[rows] = 1.0 / total
        inverse_one.append((table * weight).T)
        angle = turn * ((k1[:, None] * n2[None, :]) % total) / total
        angle[0] = 0.0
        cosines.append(np.cos(angle))
        sines.append(-np.sin(angle))
    angle = turn * ((n2[:, None] * n2[None, :]) % LANES) / LANES
    cosine, sine = np.cos(angle), np.sin(angle)
    forward_two = np.block([[cosine, -sine], [sine, cosine]])
    inverse_two = np.block([[cosine, sine], [-sine, cosine]])
    half_lanes = LANES // 2
    even = turn * ((n2[:, None] * np.arange(half_lanes)[None, :]) % LANES) / LANES
    odd = turn * ((n2[:, None] * (1 + 2 * np.arange(half_lanes))[None, :]) % (2 * LANES)) / (2 * LANES)
    zero = np.zeros((LANES, half_lanes))
    even_imag = -np.sin(even)
    even_imag[:, 0] = np.cos(np.pi * n2)
    forward_row = np.block(
        [[np.cos(even), zero, even_imag, zero], [zero, np.cos(odd), zero, -np.sin(odd)]]
    )
    weight = np.full((2 * LANES, 1), 2.0)
    weight[0] = weight[LANES] = 1.0
    inverse_row = (forward_row * weight[:, 0][None, :]).T

    def along_rows(table):
        high, low = split_table(table)
        return np.concatenate([high, low, high], axis=0)

    def along_columns(table):
        high, low = split_table(table)
        return np.concatenate([high, low, high], axis=1)

    def two_columns(table):
        return np.concatenate(split_table(table), axis=1)

    return {
        "forward_one": np.stack([two_columns(t) for t in forward_one]),
        "inverse_one": np.stack([along_columns(t) for t in inverse_one]),
        "turns": np.stack([cosines, sines], axis=1).astype(np.float32),
        "forward_two": along_rows(forward_two),
        "inverse_two": along_rows(inverse_two),
        "forward_row": along_rows(forward_row),
        "inverse_row": along_rows(inverse_row),
    }


def prep_kernel(signal, gate, mix, result, raw, turned, data, landed, left):
    step = raw.shape[1] // LANES
    channels = raw.shape[2]
    rows = data.shape[1] // 2
    copies = [
        pltpu.make_async_copy(source, raw.at[i], landed.at[i])
        for i, source in enumerate((signal, gate, mix))
    ]
    for copy in copies:
        copy.start()
    writes = []
    for part in range(2):
        for copy in copies[1:] if part else copies[:1]:
            copy.wait()
        for t in range(step):
            piece = pl.ds(t * LANES, LANES)
            if part == 0:
                value = raw[0, piece, :].astype(F32)
            else:
                value = raw[1, piece, :].astype(F32) * raw[2, piece, :].astype(F32)
            turned[pl.ds(t, channels, stride=step), :] = value.T
        half = (slice(None), pl.ds(part * rows, rows))
        data[half] = turned[: channels * step].reshape(data.shape[0], rows, LANES).astype(BF16)
        writes.append(pltpu.make_async_copy(data.at[half], result.at[half], left.at[part]))
        writes[part].start()
    for write in writes:
        write.wait()


def place():
    n = lax.axis_size("ctx")
    me = lax.axis_index("ctx")
    peers = n // 2
    return me, me // peers, lax.rem(me, peers), me == 0, me == peers


def sent_blocks(peers, parity):
    chips = [[s, s + 1] for s in range(2, peers // 2, 2)]
    return [[0], [1]] + chips + [[s + parity] for s in range(peers // 2, peers, 2)]


def held_blocks(peers, parity):
    received = [offsets[0] for offsets in sent_blocks(peers, parity)]
    beside = list(range(3, peers // 2, 2))
    return received + beside + [s + 1 - parity for s in range(peers // 2, peers, 2)]


def special_kernel(spec_one, spec_two, *refs):
    *outs, raw, strided, turned, landed = refs
    parity = lax.rem(lax.axis_index("group"), 2)
    step = spec_one.shape[2] // LANES
    lines = step // 2
    width = raw.shape[3]
    _, half, _, is_first, _ = place()
    columns = pl.ds(pl.multiple_of((1 - half) * width, width), width)
    copies = [
        pltpu.make_async_copy(spec.at[ri, 0, :, columns], raw.at[index, ri], landed.at[index, ri])
        for index, spec in enumerate((spec_one, spec_two))
        for ri in range(2)
    ]
    for copy in copies:
        copy.start()
    for index in range(2):
        for ri in range(2):
            copies[2 * index + ri].wait()
            strided[ri, : raw.shape[2]] = raw[index, ri].astype(F32)
        for j in range(lines):
            pair = [strided[ri, pl.ds(j, LANES, stride=step), :] for ri in range(2)]
            if j == 0:
                packed = pack_row(strided, pair[0], pair[1], step)
                pair = [jnp.where(is_first, p, v) for p, v in zip(packed, pair)]
            for ri in range(2):
                turned[index, pl.ds(ri * lines + j, width, stride=step), :] = pair[ri].T
        size = outs[0].shape[2]
        for i, out in enumerate(outs):
            for core in range(2):
                begin = pl.multiple_of((4 * i + 2 * parity + core) * size, size)
                out[core, index] = turned[index, pl.ds(begin, size), :].astype(BF16)


def pack_row(strided, real_part, imag_part, step):
    half = LANES // 2
    odd = [strided[ri, pl.ds(step // 2, LANES, stride=step), :] for ri in range(2)]
    packed_real = jnp.concatenate([real_part[:half], odd[0][:half]], axis=0)
    packed_imag = jnp.concatenate([imag_part[:half], odd[1][:half]], axis=0)
    top = lax.broadcasted_iota(jnp.int32, packed_imag.shape, 0) == 0
    middle = jnp.broadcast_to(real_part[half : half + 1], packed_imag.shape)
    return packed_real, jnp.where(top, middle, packed_imag)


def pack_kernel(spec_one, spec_two, *refs):
    *outs, raw, strided, turned, landed, other_raw, other_turned, other_landed = refs
    peers = lax.axis_size("ctx") // 2
    lacked, outs = outs[-(peers // 4) :], outs[: -(peers // 4)]
    step = spec_one.shape[2] // LANES
    channels = raw.shape[4]
    _, half, low_index, is_first, is_middle = place()
    parity = lax.rem(lax.axis_index("group"), 2)
    row_count = 2 * step
    columns = pl.ds(pl.multiple_of(half * channels, channels), channels)
    copies = {
        (index, a, ri): pltpu.make_async_copy(
            spec.at[ri, a, :, columns], raw.at[index, a, ri], landed.at[index, a, ri]
        )
        for index, spec in enumerate((spec_one, spec_two))
        for a in range(2)
        for ri in range(2)
    }
    for copy in copies.values():
        copy.start()
    special_kernel(
        spec_one, spec_two, *lacked, other_raw, strided, other_turned, other_landed
    )
    for index in range(2):
        for a in range(2):
            for ri in range(2):
                copies[index, a, ri].wait()
                strided[ri, : raw.shape[3]] = raw[index, a, ri].astype(F32)
            for low in range(step):
                pair = [strided[ri, pl.ds(low, LANES, stride=step), :] for ri in range(2)]
                if a == 0 and low == 0:
                    packed = pack_row(strided, pair[0], pair[1], step)
                    pair = [jnp.where(is_first, p, v) for p, v in zip(packed, pair)]
                for ri in range(2):
                    value = pair[ri]
                    if a == 0 and low >= step // 2:
                        own = strided[ri, pl.ds(low - step // 2, LANES, stride=step), :]
                        value = jnp.where(is_middle, own, value)
                    row = ri * row_count + a * step + low
                    turned[pl.ds(row, channels, stride=2 * row_count), :] = value.T
        block = channels // peers * 2 * row_count
        for offsets, out in zip(sent_blocks(peers, parity), outs):
            for i, s in enumerate(offsets):
                start = pl.multiple_of((low_index ^ s) * block, block)
                out[i, index] = turned[pl.ds(start, block), :].astype(BF16)


def split_value(value):
    high = value.astype(BF16)
    return high, (value - high.astype(F32)).astype(BF16)


def split_columns(value):
    high, low = split_value(value)
    return jnp.concatenate([high, high, low], axis=1)


def split_rows(value):
    high, low = split_value(value)
    return jnp.concatenate([high, high, low], axis=0)


def dot(left, right):
    return jnp.dot(left, right, preferred_element_type=F32)


def insert_rows(filters, lacking, half, step):
    lines = step // 2
    shape = (filters.shape[2] // (4 * step), 4 * step, LANES)
    for index in range(2):
        own = lacking[index].astype(F32)
        size = own.shape[0]
        before, after = pltpu.roll(own, lines, 0), pltpu.roll(own, size - lines, 0)
        row = lax.rem(lax.broadcasted_iota(jnp.int32, own.shape, 0), step)
        low = row < lines
        chosen = (low == (half == 1)).reshape(-1, step, LANES)
        real_part = jnp.where(low, own, before).reshape(-1, step, LANES)
        imag_part = jnp.where(low, after, own).reshape(-1, step, LANES)
        old = filters[0, index].astype(F32).reshape(shape)
        new = jnp.concatenate(
            [
                jnp.where(chosen, real_part, old[:, :step]),
                old[:, step : 2 * step],
                jnp.where(chosen, imag_part, old[:, 2 * step : 3 * step]),
                old[:, 3 * step :],
            ],
            axis=1,
        )
        filters[0, index] = new.reshape(filters.shape[2:]).astype(BF16)


HALVED = ("forward_one", "turns", "inverse_one")
PARTS = ("data", "forward_one", "turns", "forward_two", "forward_row")
LATER = ("inverse_two", "inverse_row", "inverse_one")


def conv_kernel(peers, skip_one, skip_two, *refs):
    names = PARTS + LATER
    sources = dict(zip(names, refs))
    blocks, refs = refs[len(names) : len(names) + peers], refs[len(names) + peers :]
    specials, result, refs = refs[:2], refs[2], refs[3:]
    buffers = dict(zip(names, refs))
    filters, lacking, out, landed, left = refs[len(names) :]
    me, half, low_index, _, _ = place()
    copies = {}
    for i, name in enumerate(names):
        source = sources[name].at[half] if name in HALVED else sources[name]
        copies[name] = pltpu.make_async_copy(source, buffers[name], landed.at[i])
    parity = lax.rem(lax.axis_index("group"), 2)
    for i, s in enumerate(held_blocks(peers, parity)):
        copies[i] = pltpu.make_async_copy(
            blocks[i].at[0], filters.at[low_index ^ s], landed.at[len(names) + i]
        )
    for name in PARTS:
        copies[name].start()
    for core, special in enumerate(specials):
        copies["special"] = pltpu.make_async_copy(special, lacking, landed.at[len(names) + peers])

        @pl.when(lax.rem(me, 2) == core)
        def _():
            copies["special"].start()

    for name in tuple(range(peers)) + LATER:
        copies[name].start()
    awaited = set()

    def need(*wanted):
        for name in wanted:
            if name not in awaited:
                awaited.add(name)
                copies[name].wait()

    data, turns = buffers["data"], buffers["turns"]
    devices = data.shape[0]
    per_device = out.shape[1]
    rows = turns.shape[1]
    step = rows // devices
    count = per_device // step
    row_count = 2 * step
    top_row = lax.broadcasted_iota(jnp.int32, (step, 2 * LANES), 0) == 0
    corner = top_row[:, :LANES] & (lax.broadcasted_iota(jnp.int32, (step, LANES), 1) == 0)

    def with_top(values, tops):
        return [
            jnp.concatenate(
                [jnp.where(top_row, tops[c * step : (c + 1) * step], v[:step]), v[step:]], axis=0
            )
            for c, v in enumerate(values)
        ]

    def second_stage(values, table, row_table):
        need(table, row_table)
        main = dot(split_columns(jnp.concatenate(values, axis=0)), buffers[table][...])
        tops = dot(split_columns(jnp.concatenate([v[:step] for v in values], axis=0)), buffers[row_table][...])
        return with_top([main[c * rows : (c + 1) * rows] for c in range(GROUP)], tops)

    def convolve(fields, layer, first):
        joined = jnp.concatenate(fields, axis=1)
        need("forward_one", "turns")
        cosine, sine = turns[0], turns[1]
        staged = dot(buffers["forward_one"][...], jnp.concatenate([joined, joined], axis=0))
        turned = []
        for c in range(GROUP):
            lanes = slice(c * LANES, (c + 1) * LANES)
            real_part, imag_part = staged[:rows, lanes], staged[rows:, lanes]
            turned.append(
                jnp.concatenate(
                    [
                        real_part * cosine - imag_part * sine,
                        real_part * sine + imag_part * cosine,
                    ],
                    axis=1,
                )
            )
        spectral = second_stage(turned, "forward_two", "forward_row")
        if "special" not in awaited:
            need("special", *range(peers))
            insert_rows(filters, lacking, half, step)
        products = []
        for c in range(GROUP):
            start = (first + c) * 2 * row_count
            stored = filters[:, layer, start : start + 2 * row_count, :]
            h_real = stored[:, :row_count].reshape(rows, LANES).astype(F32)
            h_imag = stored[:, row_count:].reshape(rows, LANES).astype(F32)
            x_real, x_imag = spectral[c][:, :LANES], spectral[c][:, LANES:]
            real_real, imag_imag = x_real * h_real, x_imag * h_imag
            y_real = real_real - imag_imag
            y_imag = x_real * h_imag + x_imag * h_real
            y_real = jnp.concatenate(
                [jnp.where(corner, real_real[:step], y_real[:step]), y_real[step:]], axis=0
            )
            y_imag = jnp.concatenate(
                [jnp.where(corner, imag_imag[:step], y_imag[:step]), y_imag[step:]], axis=0
            )
            products.append(jnp.concatenate([y_real, y_imag], axis=1))
        inverted = second_stage(products, "inverse_two", "inverse_row")
        columns = []
        for c in range(GROUP):
            real_part, imag_part = inverted[c][:, :LANES], inverted[c][:, LANES:]
            columns.append(
                jnp.concatenate(
                    [
                        real_part * cosine + imag_part * sine,
                        imag_part * cosine - real_part * sine,
                    ],
                    axis=0,
                )
            )
        need("inverse_one")
        result = dot(buffers["inverse_one"][...], split_rows(jnp.concatenate(columns, axis=1)))
        return [result[:, c * LANES : (c + 1) * LANES] for c in range(GROUP)]

    need("data")
    size = GROUP * step
    writes = []
    for first in range(0, count, GROUP):

        def channels(start):
            values = data[:, start : start + size, :].astype(F32)
            return [
                values[:, c * step : (c + 1) * step, :].reshape(rows, LANES) for c in range(GROUP)
            ]

        base = first * step
        place_of = me * count + first
        fields = channels(base)
        results = convolve([f.astype(BF16) for f in fields], 0, first)
        middles = [
            (g * (r + skip_one[place_of + c] * f)).astype(BF16)
            for c, (g, r, f) in enumerate(zip(channels(per_device + base), results, fields))
        ]
        results = convolve(middles, 1, first)
        results = [
            (r + skip_two[place_of + c] * m.astype(F32)).reshape(devices, step, LANES)
            for c, (r, m) in enumerate(zip(results, middles))
        ]
        out[:, base : base + size, :] = jnp.concatenate(results, axis=1).astype(BF16)
        part = (slice(None), pl.ds(base, size))
        writes.append(pltpu.make_async_copy(out.at[part], result.at[part], left.at[len(writes)]))
        writes[-1].start()
    for write in writes:
        write.wait()


def final_kernel(back, gate, out, turned):
    step = gate.shape[0] // LANES
    channels = gate.shape[1]
    turned[: channels * step] = back[...].astype(F32).reshape(channels * step, LANES)
    for t in range(step):
        piece = pl.ds(t * LANES, LANES)
        value = turned[pl.ds(t, channels, stride=step), :].T
        out[piece, :] = (gate[piece, :].astype(F32) * value).astype(BF16)


ANY = pl.BlockSpec(memory_space=pl.ANY)
VMEM = pl.BlockSpec(memory_space=pltpu.VMEM)


def run_convolve(skips, data, blocks, specials, tables, n, step, count):
    peers = n // 2
    per_device = count * step
    operands = dict(tables, data=data)
    operands = [operands[name] for name in PARTS + LATER]
    buffers = [
        pltpu.VMEM(o.shape[1:] if name in HALVED else o.shape, o.dtype)
        for name, o in zip(PARTS + LATER, operands)
    ]
    return pl.pallas_call(
        functools.partial(conv_kernel, peers),
        in_specs=[pl.BlockSpec(memory_space=pltpu.SMEM)] * 2 + [ANY] * (len(operands) + peers + 2),
        out_specs=ANY,
        out_shape=jax.ShapeDtypeStruct((n, per_device, LANES), BF16),
        scratch_shapes=buffers
        + [
            pltpu.VMEM((peers,) + blocks[0].shape[1:], BF16),
            pltpu.VMEM(specials[0].shape, BF16),
            pltpu.VMEM((n, per_device, LANES), BF16),
            pltpu.SemaphoreType.DMA((len(operands) + peers + 1,)),
            pltpu.SemaphoreType.DMA((count // GROUP,)),
        ],
        compiler_params=PARAMS,
        cost_estimate=pl.CostEstimate(
            flops=2400 * 1000 * 1000, bytes_accessed=8 * 1024 * 1024, transcendentals=0
        ),
        name="convolve",
    )(*skips, *operands, *blocks, *specials)


def on_device(signal, gate_one, mix_two, gate_two, skip_one, skip_two, spectrum_one, spectrum_two):
    n = lax.axis_size("ctx")
    groups = lax.axis_size("group")
    peers = n // 2
    length, channels = signal.shape
    step = length // LANES
    count = channels // n
    per_device = count * step
    half_channels = channels // 2

    data_shape = (n, 2 * per_device, LANES)
    data = pl.pallas_call(
        prep_kernel,
        in_specs=[ANY] * 3,
        out_specs=ANY,
        out_shape=jax.ShapeDtypeStruct(data_shape, BF16),
        scratch_shapes=[
            pltpu.VMEM((3, length, channels), BF16),
            pltpu.VMEM(((channels + 1) * step, LANES), F32),
            pltpu.VMEM(data_shape, BF16),
            pltpu.SemaphoreType.DMA((3,)),
            pltpu.SemaphoreType.DMA((2,)),
        ],
        compiler_params=PARAMS,
        name="prep",
    )(signal, gate_one, mix_two)

    both = ("group", "ctx")
    block_shape = (2, count * 4 * step, LANES)
    shapes = [(len(offsets),) + block_shape for offsets in sent_blocks(peers, 0)]
    lacked_shape = jax.ShapeDtypeStruct((2, 2, per_device, LANES), BF16)
    turned = pl.pallas_call(
        pack_kernel,
        in_specs=[ANY, ANY],
        out_specs=[VMEM] * (len(shapes) + peers // 4),
        out_shape=[jax.ShapeDtypeStruct(shape, BF16) for shape in shapes]
        + [lacked_shape] * (peers // 4),
        scratch_shapes=[
            pltpu.VMEM((2, 2, 2, length, half_channels), BF16),
            pltpu.VMEM((2, length + step, half_channels), F32),
            pltpu.VMEM(((half_channels + 1) * 4 * step, LANES), F32),
            pltpu.SemaphoreType.DMA((2, 2, 2)),
            pltpu.VMEM((2, 2, length, half_channels), BF16),
            pltpu.VMEM((2, (half_channels + 1) * step, LANES), F32),
            pltpu.SemaphoreType.DMA((2, 2)),
        ],
        compiler_params=PARAMS,
        name="pack",
    )(spectrum_one, spectrum_two)
    blocks, lacked = turned[: len(shapes)], turned[len(shapes) :]
    routes = [[offsets[0] for offsets in sent_blocks(peers, g % 2)] for g in range(groups)]
    received = [
        lax.ppermute(
            block, both, [(g * n + d, g * n + (d ^ routes[g][i])) for g in range(groups) for d in range(n)]
        )
        if i
        else block
        for i, block in enumerate(blocks)
    ]
    mates = [(d, d ^ 1) for d in range(n)]
    swap = [(g, g ^ 1) for g in range(groups)]
    far = 1 + peers // 4
    passed = [lax.ppermute(block, "group", swap) for block in received[far:]]
    beside = [lax.ppermute(block[1:], "ctx", mates) for block in received[2:far]]

    lacked = [
        lax.ppermute(
            rows,
            both,
            [
                (g * n + peers - end, g * n + end + 4 * i + 2 * (g % 2))
                for g in range(groups)
                for end in (0, peers)
            ],
        )
        for i, rows in enumerate(lacked)
    ]
    lacked = sum(lacked[1:], lacked[0])
    holders = [(g, d) for g in range(groups) for d in range(0, n, 2) if d // 2 % 2 == g % 2]
    others = lax.ppermute(lacked, both, [(g * n + d, (g ^ 1) * n + d) for g, d in holders])
    others, passed[0] = lax.optimization_barrier((others, passed[0]))
    lacked = lacked + others
    mine = (lacked[0], lax.ppermute(lacked[1], "ctx", [(d, d + 1) for d in range(0, n, 2)]))
    data = lax.all_to_all(data, "ctx", split_axis=0, concat_axis=0, tiled=True)
    held = received + beside + passed
    tables = {name: jnp.asarray(table) for name, table in make_tables(n, step).items()}
    skips = (skip_one, skip_two)
    out = run_convolve(skips, data, held, mine, tables, n, step, count)
    back = lax.all_to_all(out, "ctx", split_axis=0, concat_axis=0, tiled=True)
    return pl.pallas_call(
        final_kernel,
        out_shape=jax.ShapeDtypeStruct((length, channels), BF16),
        scratch_shapes=[pltpu.VMEM(((channels + 1) * step, LANES), F32)],
        compiler_params=SMALL,
        name="final",
    )(back, gate_two)


def solution(mesh):
    return jax.shard_map(
        on_device,
        mesh=mesh,
        in_specs=(
            P(("group", "ctx"), None),
            P(("group", "ctx"), None),
            P(("group", "ctx"), None),
            P(("group", "ctx"), None),
            P(),
            P(),
            P(None, "ctx", None, None),
            P(None, "ctx", None, None),
        ),
        out_specs=P(("group", "ctx"), None),
        check_vma=False,
    )
```

```python
import functools

import jax
import jax.numpy as jnp
import numpy as np
from jax import lax
from jax.experimental import pallas as pl
from jax.experimental.pallas import tpu as pltpu
from jax.sharding import PartitionSpec as P

F32 = jnp.float32
BF16 = jnp.bfloat16
LANES = 128
GROUP = 8
SMALL = pltpu.CompilerParams(vmem_limit_bytes=24 * 1024 * 1024)
PARAMS = pltpu.CompilerParams(vmem_limit_bytes=60 * 1024 * 1024)


def split_table(table):
    high = table.astype(jnp.bfloat16)
    low = (table - high.astype(np.float64)).astype(jnp.bfloat16)
    return high, low


def make_tables(n, step):
    rows = n * step
    first_len = 2 * rows
    total = first_len * LANES
    turn = 2.0 * np.pi
    n1 = np.arange(rows)
    n2 = np.arange(LANES)
    forward_one, inverse_one, cosines, sines = [], [], [], []
    for half in range(2):
        k1 = np.array(
            [
                2 * (half * (n // 2) + source) + a + 2 * n * low
                for source in range(n // 2)
                for a in range(2)
                for low in range(step)
            ]
        )
        k1[:step] = [2 * n * j for j in range(step // 2)] + [n + 2 * n * j for j in range(step // 2)]
        angle = turn * ((k1[:, None] * n1[None, :]) % first_len) / first_len
        real_rows, imag_rows = np.cos(angle), -np.sin(angle)
        imag_rows[0] = np.cos(np.pi * n1)
        table = np.concatenate([real_rows, imag_rows], axis=0)
        forward_one.append(table)
        weight = np.full((2 * rows, 1), 2.0 / total)
        weight[0] = weight[rows] = 1.0 / total
        inverse_one.append((table * weight).T)
        angle = turn * ((k1[:, None] * n2[None, :]) % total) / total
        angle[0] = 0.0
        cosines.append(np.cos(angle))
        sines.append(-np.sin(angle))
    angle = turn * ((n2[:, None] * n2[None, :]) % LANES) / LANES
    cosine, sine = np.cos(angle), np.sin(angle)
    forward_two = np.block([[cosine, -sine], [sine, cosine]])
    inverse_two = np.block([[cosine, sine], [-sine, cosine]])
    half_lanes = LANES // 2
    even = turn * ((n2[:, None] * np.arange(half_lanes)[None, :]) % LANES) / LANES
    odd = turn * ((n2[:, None] * (1 + 2 * np.arange(half_lanes))[None, :]) % (2 * LANES)) / (2 * LANES)
    zero = np.zeros((LANES, half_lanes))
    even_imag = -np.sin(even)
    even_imag[:, 0] = np.cos(np.pi * n2)
    forward_row = np.block(
        [[np.cos(even), zero, even_imag, zero], [zero, np.cos(odd), zero, -np.sin(odd)]]
    )
    weight = np.full((2 * LANES, 1), 2.0)
    weight[0] = weight[LANES] = 1.0
    inverse_row = (forward_row * weight[:, 0][None, :]).T

    def along_rows(table):
        high, low = split_table(table)
        return np.concatenate([high, low, high], axis=0)

    def along_columns(table):
        high, low = split_table(table)
        return np.concatenate([high, low, high], axis=1)

    def two_columns(table):
        return np.concatenate(split_table(table), axis=1)

    return {
        "forward_one": np.stack([two_columns(t) for t in forward_one]),
        "inverse_one": np.stack([along_columns(t) for t in inverse_one]),
        "turns": np.stack([cosines, sines], axis=1).astype(np.float32),
        "forward_two": along_rows(forward_two),
        "inverse_two": along_rows(inverse_two),
        "forward_row": along_rows(forward_row),
        "inverse_row": along_rows(inverse_row),
    }


def prep_kernel(signal, gate, mix, result, raw, turned, data, landed, left):
    step = raw.shape[1] // LANES
    channels = raw.shape[2]
    rows = data.shape[1] // 2
    copies = [
        pltpu.make_async_copy(source, raw.at[i], landed.at[i])
        for i, source in enumerate((signal, gate, mix))
    ]
    for copy in copies:
        copy.start()
    writes = []
    for part in range(2):
        for copy in copies[1:] if part else copies[:1]:
            copy.wait()
        for t in range(step):
            piece = pl.ds(t * LANES, LANES)
            if part == 0:
                value = raw[0, piece, :].astype(F32)
            else:
                value = raw[1, piece, :].astype(F32) * raw[2, piece, :].astype(F32)
            turned[pl.ds(t, channels, stride=step), :] = value.T
        half = (slice(None), pl.ds(part * rows, rows))
        data[half] = turned[: channels * step].reshape(data.shape[0], rows, LANES).astype(BF16)
        writes.append(pltpu.make_async_copy(data.at[half], result.at[half], left.at[part]))
        writes[part].start()
    for write in writes:
        write.wait()


def place():
    n = lax.axis_size("ctx")
    me = lax.axis_index("ctx")
    peers = n // 2
    return me, me // peers, lax.rem(me, peers), me == 0, me == peers


def sent_blocks(peers, parity):
    chips = [[s, s + 1] for s in range(2, peers // 2, 2)]
    return [[0], [1]] + chips + [[s + parity] for s in range(peers // 2, peers, 2)]


def held_blocks(peers, parity):
    received = [offsets[0] for offsets in sent_blocks(peers, parity)]
    beside = list(range(3, peers // 2, 2))
    return received + beside + [s + 1 - parity for s in range(peers // 2, peers, 2)]


def special_kernel(spec_one, spec_two, *refs):
    *outs, raw, strided, turned, landed = refs
    parity = lax.rem(lax.axis_index("group"), 2)
    step = spec_one.shape[2] // LANES
    lines = step // 2
    width = raw.shape[3]
    _, half, _, is_first, _ = place()
    columns = pl.ds(pl.multiple_of((1 - half) * width, width), width)
    copies = [
        pltpu.make_async_copy(spec.at[ri, 0, :, columns], raw.at[index, ri], landed.at[index, ri])
        for index, spec in enumerate((spec_one, spec_two))
        for ri in range(2)
    ]
    for copy in copies:
        copy.start()
    for index in range(2):
        for ri in range(2):
            copies[2 * index + ri].wait()
            strided[ri, : raw.shape[2]] = raw[index, ri].astype(F32)
        for j in range(lines):
            pair = [strided[ri, pl.ds(j, LANES, stride=step), :] for ri in range(2)]
            if j == 0:
                packed = pack_row(strided, pair[0], pair[1], step)
                pair = [jnp.where(is_first, p, v) for p, v in zip(packed, pair)]
            for ri in range(2):
                turned[index, pl.ds(ri * lines + j, width, stride=step), :] = pair[ri].T
        size = outs[0].shape[2]
        for i, out in enumerate(outs):
            for core in range(2):
                begin = pl.multiple_of((4 * i + 2 * parity + core) * size, size)
                out[core, index] = turned[index, pl.ds(begin, size), :].astype(BF16)


def pack_row(strided, real_part, imag_part, step):
    half = LANES // 2
    odd = [strided[ri, pl.ds(step // 2, LANES, stride=step), :] for ri in range(2)]
    packed_real = jnp.concatenate([real_part[:half], odd[0][:half]], axis=0)
    packed_imag = jnp.concatenate([imag_part[:half], odd[1][:half]], axis=0)
    top = lax.broadcasted_iota(jnp.int32, packed_imag.shape, 0) == 0
    middle = jnp.broadcast_to(real_part[half : half + 1], packed_imag.shape)
    return packed_real, jnp.where(top, middle, packed_imag)


def pack_kernel(spec_one, spec_two, *refs):
    *outs, raw, strided, turned, landed, other_raw, other_turned, other_landed = refs
    peers = lax.axis_size("ctx") // 2
    lacked, outs = outs[-(peers // 4) :], outs[: -(peers // 4)]
    step = spec_one.shape[2] // LANES
    channels = raw.shape[4]
    _, half, low_index, is_first, is_middle = place()
    parity = lax.rem(lax.axis_index("group"), 2)
    row_count = 2 * step
    columns = pl.ds(pl.multiple_of(half * channels, channels), channels)
    copies = {
        (index, a, ri): pltpu.make_async_copy(
            spec.at[ri, a, :, columns], raw.at[index, a, ri], landed.at[index, a, ri]
        )
        for index, spec in enumerate((spec_one, spec_two))
        for a in range(2)
        for ri in range(2)
    }
    for copy in copies.values():
        copy.start()
    special_kernel(
        spec_one, spec_two, *lacked, other_raw, strided, other_turned, other_landed
    )
    for index in range(2):
        for a in range(2):
            for ri in range(2):
                copies[index, a, ri].wait()
                strided[ri, : raw.shape[3]] = raw[index, a, ri].astype(F32)
            for low in range(step):
                pair = [strided[ri, pl.ds(low, LANES, stride=step), :] for ri in range(2)]
                if a == 0 and low == 0:
                    packed = pack_row(strided, pair[0], pair[1], step)
                    pair = [jnp.where(is_first, p, v) for p, v in zip(packed, pair)]
                for ri in range(2):
                    value = pair[ri]
                    if a == 0 and low >= step // 2:
                        own = strided[ri, pl.ds(low - step // 2, LANES, stride=step), :]
                        value = jnp.where(is_middle, own, value)
                    row = ri * row_count + a * step + low
                    turned[pl.ds(row, channels, stride=2 * row_count), :] = value.T
        block = channels // peers * 2 * row_count
        for offsets, out in zip(sent_blocks(peers, parity), outs):
            for i, s in enumerate(offsets):
                start = pl.multiple_of((low_index ^ s) * block, block)
                out[i, index] = turned[pl.ds(start, block), :].astype(BF16)


def split_value(value):
    high = value.astype(BF16)
    return high, (value - high.astype(F32)).astype(BF16)


def split_columns(value):
    high, low = split_value(value)
    return jnp.concatenate([high, high, low], axis=1)


def split_rows(value):
    high, low = split_value(value)
    return jnp.concatenate([high, high, low], axis=0)


def dot(left, right):
    return jnp.dot(left, right, preferred_element_type=F32)


def insert_rows(filters, lacking, half, step):
    lines = step // 2
    shape = (filters.shape[2] // (4 * step), 4 * step, LANES)
    for index in range(2):
        own = lacking[index].astype(F32)
        size = own.shape[0]
        before, after = pltpu.roll(own, lines, 0), pltpu.roll(own, size - lines, 0)
        row = lax.rem(lax.broadcasted_iota(jnp.int32, own.shape, 0), step)
        low = row < lines
        chosen = (low == (half == 1)).reshape(-1, step, LANES)
        real_part = jnp.where(low, own, before).reshape(-1, step, LANES)
        imag_part = jnp.where(low, after, own).reshape(-1, step, LANES)
        old = filters[0, index].astype(F32).reshape(shape)
        new = jnp.concatenate(
            [
                jnp.where(chosen, real_part, old[:, :step]),
                old[:, step : 2 * step],
                jnp.where(chosen, imag_part, old[:, 2 * step : 3 * step]),
                old[:, 3 * step :],
            ],
            axis=1,
        )
        filters[0, index] = new.reshape(filters.shape[2:]).astype(BF16)


HALVED = ("forward_one", "turns", "inverse_one")
PARTS = ("data", "forward_one", "turns", "forward_two", "forward_row")
LATER = ("inverse_two", "inverse_row", "inverse_one")


def conv_kernel(peers, skip_one, skip_two, *refs):
    names = PARTS + LATER
    sources = dict(zip(names, refs))
    blocks, refs = refs[len(names) : len(names) + peers], refs[len(names) + peers :]
    specials, result, refs = refs[:2], refs[2], refs[3:]
    buffers = dict(zip(names, refs))
    filters, lacking, out, landed, left = refs[len(names) :]
    me, half, low_index, _, _ = place()
    copies = {}
    for i, name in enumerate(names):
        source = sources[name].at[half] if name in HALVED else sources[name]
        copies[name] = pltpu.make_async_copy(source, buffers[name], landed.at[i])
    parity = lax.rem(lax.axis_index("group"), 2)
    for i, s in enumerate(held_blocks(peers, parity)):
        copies[i] = pltpu.make_async_copy(
            blocks[i].at[0], filters.at[low_index ^ s], landed.at[len(names) + i]
        )
    for name in PARTS:
        copies[name].start()
    for core, special in enumerate(specials):
        copies["special"] = pltpu.make_async_copy(special, lacking, landed.at[len(names) + peers])

        @pl.when(lax.rem(me, 2) == core)
        def _():
            copies["special"].start()

    for name in tuple(range(peers)) + LATER:
        copies[name].start()
    awaited = set()

    def need(*wanted):
        for name in wanted:
            if name not in awaited:
                awaited.add(name)
                copies[name].wait()

    data, turns = buffers["data"], buffers["turns"]
    devices = data.shape[0]
    per_device = out.shape[1]
    rows = turns.shape[1]
    step = rows // devices
    count = per_device // step
    row_count = 2 * step
    top_row = lax.broadcasted_iota(jnp.int32, (step, 2 * LANES), 0) == 0
    corner = top_row[:, :LANES] & (lax.broadcasted_iota(jnp.int32, (step, LANES), 1) == 0)

    def with_top(values, tops):
        return [
            jnp.concatenate(
                [jnp.where(top_row, tops[c * step : (c + 1) * step], v[:step]), v[step:]], axis=0
            )
            for c, v in enumerate(values)
        ]

    def second_stage(values, table, row_table):
        need(table, row_table)
        main = dot(split_columns(jnp.concatenate(values, axis=0)), buffers[table][...])
        tops = dot(split_columns(jnp.concatenate([v[:step] for v in values], axis=0)), buffers[row_table][...])
        return with_top([main[c * rows : (c + 1) * rows] for c in range(GROUP)], tops)

    def convolve(fields, layer, first):
        joined = jnp.concatenate(fields, axis=1)
        need("forward_one", "turns")
        cosine, sine = turns[0], turns[1]
        staged = dot(buffers["forward_one"][...], jnp.concatenate([joined, joined], axis=0))
        turned = []
        for c in range(GROUP):
            lanes = slice(c * LANES, (c + 1) * LANES)
            real_part, imag_part = staged[:rows, lanes], staged[rows:, lanes]
            turned.append(
                jnp.concatenate(
                    [
                        real_part * cosine - imag_part * sine,
                        real_part * sine + imag_part * cosine,
                    ],
                    axis=1,
                )
            )
        spectral = second_stage(turned, "forward_two", "forward_row")
        if "special" not in awaited:
            need("special", *range(peers))
            insert_rows(filters, lacking, half, step)
        products = []
        for c in range(GROUP):
            start = (first + c) * 2 * row_count
            stored = filters[:, layer, start : start + 2 * row_count, :]
            h_real = stored[:, :row_count].reshape(rows, LANES).astype(F32)
            h_imag = stored[:, row_count:].reshape(rows, LANES).astype(F32)
            x_real, x_imag = spectral[c][:, :LANES], spectral[c][:, LANES:]
            real_real, imag_imag = x_real * h_real, x_imag * h_imag
            y_real = real_real - imag_imag
            y_imag = x_real * h_imag + x_imag * h_real
            y_real = jnp.concatenate(
                [jnp.where(corner, real_real[:step], y_real[:step]), y_real[step:]], axis=0
            )
            y_imag = jnp.concatenate(
                [jnp.where(corner, imag_imag[:step], y_imag[:step]), y_imag[step:]], axis=0
            )
            products.append(jnp.concatenate([y_real, y_imag], axis=1))
        inverted = second_stage(products, "inverse_two", "inverse_row")
        columns = []
        for c in range(GROUP):
            real_part, imag_part = inverted[c][:, :LANES], inverted[c][:, LANES:]
            columns.append(
                jnp.concatenate(
                    [
                        real_part * cosine + imag_part * sine,
                        imag_part * cosine - real_part * sine,
                    ],
                    axis=0,
                )
            )
        need("inverse_one")
        result = dot(buffers["inverse_one"][...], split_rows(jnp.concatenate(columns, axis=1)))
        return [result[:, c * LANES : (c + 1) * LANES] for c in range(GROUP)]

    need("data")
    size = GROUP * step
    writes = []
    for first in range(0, count, GROUP):

        def channels(start):
            values = data[:, start : start + size, :].astype(F32)
            return [
                values[:, c * step : (c + 1) * step, :].reshape(rows, LANES) for c in range(GROUP)
            ]

        base = first * step
        place_of = me * count + first
        fields = channels(base)
        results = convolve([f.astype(BF16) for f in fields], 0, first)
        middles = [
            (g * (r + skip_one[place_of + c] * f)).astype(BF16)
            for c, (g, r, f) in enumerate(zip(channels(per_device + base), results, fields))
        ]
        results = convolve(middles, 1, first)
        results = [
            (r + skip_two[place_of + c] * m.astype(F32)).reshape(devices, step, LANES)
            for c, (r, m) in enumerate(zip(results, middles))
        ]
        out[:, base : base + size, :] = jnp.concatenate(results, axis=1).astype(BF16)
        part = (slice(None), pl.ds(base, size))
        writes.append(pltpu.make_async_copy(out.at[part], result.at[part], left.at[len(writes)]))
        writes[-1].start()
    for write in writes:
        write.wait()


def final_kernel(back, gate, out, turned):
    step = gate.shape[0] // LANES
    channels = gate.shape[1]
    turned[: channels * step] = back[...].astype(F32).reshape(channels * step, LANES)
    for t in range(step):
        piece = pl.ds(t * LANES, LANES)
        value = turned[pl.ds(t, channels, stride=step), :].T
        out[piece, :] = (gate[piece, :].astype(F32) * value).astype(BF16)


ANY = pl.BlockSpec(memory_space=pl.ANY)
VMEM = pl.BlockSpec(memory_space=pltpu.VMEM)


def run_convolve(skips, data, blocks, specials, tables, n, step, count):
    peers = n // 2
    per_device = count * step
    operands = dict(tables, data=data)
    operands = [operands[name] for name in PARTS + LATER]
    buffers = [
        pltpu.VMEM(o.shape[1:] if name in HALVED else o.shape, o.dtype)
        for name, o in zip(PARTS + LATER, operands)
    ]
    return pl.pallas_call(
        functools.partial(conv_kernel, peers),
        in_specs=[pl.BlockSpec(memory_space=pltpu.SMEM)] * 2 + [ANY] * (len(operands) + peers + 2),
        out_specs=ANY,
        out_shape=jax.ShapeDtypeStruct((n, per_device, LANES), BF16),
        scratch_shapes=buffers
        + [
            pltpu.VMEM((peers,) + blocks[0].shape[1:], BF16),
            pltpu.VMEM(specials[0].shape, BF16),
            pltpu.VMEM((n, per_device, LANES), BF16),
            pltpu.SemaphoreType.DMA((len(operands) + peers + 1,)),
            pltpu.SemaphoreType.DMA((count // GROUP,)),
        ],
        compiler_params=PARAMS,
        cost_estimate=pl.CostEstimate(
            flops=2400 * 1000 * 1000, bytes_accessed=8 * 1024 * 1024, transcendentals=0
        ),
        name="convolve",
    )(*skips, *operands, *blocks, *specials)


def on_device(signal, gate_one, mix_two, gate_two, skip_one, skip_two, spectrum_one, spectrum_two):
    n = lax.axis_size("ctx")
    groups = lax.axis_size("group")
    peers = n // 2
    length, channels = signal.shape
    step = length // LANES
    count = channels // n
    per_device = count * step
    half_channels = channels // 2

    data_shape = (n, 2 * per_device, LANES)
    data = pl.pallas_call(
        prep_kernel,
        in_specs=[ANY] * 3,
        out_specs=ANY,
        out_shape=jax.ShapeDtypeStruct(data_shape, BF16),
        scratch_shapes=[
            pltpu.VMEM((3, length, channels), BF16),
            pltpu.VMEM(((channels + 1) * step, LANES), F32),
            pltpu.VMEM(data_shape, BF16),
            pltpu.SemaphoreType.DMA((3,)),
            pltpu.SemaphoreType.DMA((2,)),
        ],
        compiler_params=PARAMS,
        name="prep",
    )(signal, gate_one, mix_two)

    both = ("group", "ctx")
    block_shape = (2, count * 4 * step, LANES)
    shapes = [(len(offsets),) + block_shape for offsets in sent_blocks(peers, 0)]
    lacked_shape = jax.ShapeDtypeStruct((2, 2, per_device, LANES), BF16)
    turned = pl.pallas_call(
        pack_kernel,
        in_specs=[ANY, ANY],
        out_specs=[VMEM] * (len(shapes) + peers // 4),
        out_shape=[jax.ShapeDtypeStruct(shape, BF16) for shape in shapes]
        + [lacked_shape] * (peers // 4),
        scratch_shapes=[
            pltpu.VMEM((2, 2, 2, length, half_channels), BF16),
            pltpu.VMEM((2, length + step, half_channels), F32),
            pltpu.VMEM(((half_channels + 1) * 4 * step, LANES), F32),
            pltpu.SemaphoreType.DMA((2, 2, 2)),
            pltpu.VMEM((2, 2, length, half_channels), BF16),
            pltpu.VMEM((2, (half_channels + 1) * step, LANES), F32),
            pltpu.SemaphoreType.DMA((2, 2)),
        ],
        compiler_params=PARAMS,
        name="pack",
    )(spectrum_one, spectrum_two)
    blocks, lacked = turned[: len(shapes)], turned[len(shapes) :]
    routes = [[offsets[0] for offsets in sent_blocks(peers, g % 2)] for g in range(groups)]
    received = [
        lax.ppermute(
            block, both, [(g * n + d, g * n + (d ^ routes[g][i])) for g in range(groups) for d in range(n)]
        )
        if i
        else block
        for i, block in enumerate(blocks)
    ]
    mates = [(d, d ^ 1) for d in range(n)]
    swap = [(g, g ^ 1) for g in range(groups)]
    far = 1 + peers // 4
    passed = [lax.ppermute(block, "group", swap) for block in received[far:]]
    beside = [lax.ppermute(block[1:], "ctx", mates) for block in received[2:far]]

    lacked = [
        lax.ppermute(
            rows,
            both,
            [
                (g * n + peers - end, g * n + end + 4 * i + 2 * (g % 2))
                for g in range(groups)
                for end in (0, peers)
            ],
        )
        for i, rows in enumerate(lacked)
    ]
    lacked = sum(lacked[1:], lacked[0])
    holders = [(g, d) for g in range(groups) for d in range(0, n, 2) if d // 2 % 2 == g % 2]
    others = lax.ppermute(lacked, both, [(g * n + d, (g ^ 1) * n + d) for g, d in holders])
    others, passed[0], received[2] = lax.optimization_barrier((others, passed[0], received[2]))
    lacked = lacked + others
    mine = (lacked[0], lax.ppermute(lacked[1], "ctx", [(d, d + 1) for d in range(0, n, 2)]))
    data = lax.all_to_all(data, "ctx", split_axis=0, concat_axis=0, tiled=True)
    held = received + beside + passed
    tables = {name: jnp.asarray(table) for name, table in make_tables(n, step).items()}
    skips = (skip_one, skip_two)
    out = run_convolve(skips, data, held, mine, tables, n, step, count)
    back = lax.all_to_all(out, "ctx", split_axis=0, concat_axis=0, tiled=True)
    return pl.pallas_call(
        final_kernel,
        out_shape=jax.ShapeDtypeStruct((length, channels), BF16),
        scratch_shapes=[pltpu.VMEM(((channels + 1) * step, LANES), F32)],
        compiler_params=SMALL,
        name="final",
    )(back, gate_two)


def solution(mesh):
    return jax.shard_map(
        on_device,
        mesh=mesh,
        in_specs=(
            P(("group", "ctx"), None),
            P(("group", "ctx"), None),
            P(("group", "ctx"), None),
            P(("group", "ctx"), None),
            P(),
            P(),
            P(None, "ctx", None, None),
            P(None, "ctx", None, None),
        ),
        out_specs=P(("group", "ctx"), None),
        check_vma=False,
    )
```
